32 devices in a mesh: die: 2 (over x), ty: 4 (over z), tx: 4 (over y, core).
Axes of the slice: x: 2, y: 2, z: 4, core: 2. Of those that a mesh axis runs over, the one named last changes fastest.
Arguments:
- raster: float32 [2, 1024, 4096], P('die', 'ty', 'tx'), may hold values from -12 to 12
- shift_pick: int32 [2, 4, 4], P('die', 'ty', 'tx'), may hold values from 0 to 7
- offsets: int32 [2, 4, 4, 2], P('die', 'ty', 'tx'), may hold values from -5 to 4
Outputs:
- next_map: float32 [2, 1024, 4096], P('die', 'ty', 'tx')
- prev_map: float32 [2, 1024, 4096], P('die', 'ty', 'tx')
The draws below stay inside these ranges and needn't reach their ends.
All inputs are finite; a program needn't handle non-finite values.
Results may differ from the reference program's by a relative error of at most 0.0003.
Values sent between devices are 32-bit elements; how exact they have to be, the bound alone decides.
No kernel may reach another device: no remote copies, remote signals or barrier semaphores. Data moves between devices by JAX's collectives and lax.ppermute only.
A program may use at most 64 MiB of HBM per device.

```python
import jax
import jax.numpy as jnp
from jax import lax

TH = 256
TW = 1024
R = 4
RG = 6
HW = 11
DIES = 2
TILE_ROWS = 4
TILE_COLS = 4
H = 1024
W = 4096


def touch_ends(entries, rng, low, largest):
    longest = entries.shape.index(max(entries.shape))
    spots = []
    for shift in (0, 1):
        where = [jax.random.randint(jax.random.fold_in(rng, axis), (), 0, length) for axis, length in enumerate(entries.shape)]
        where[longest] = (where[longest] + shift) % entries.shape[longest]
        spots.append(tuple(where))
    return entries.at[spots[0]].set(low).at[spots[1]].set(largest)


def shard_levels(rng, extent, split, smallest, top_value):
    level, own = 1.0, jax.random.fold_in(rng, 6)
    for dim, parts in split:
        steps = jnp.exp(jax.random.uniform(jax.random.fold_in(own, dim), (parts,), jnp.float32, smallest / len(split), top_value / len(split)))
        level = level * jnp.repeat(steps, extent[dim] // parts).reshape([-1 if axis == dim else 1 for axis in range(len(extent))])
    return level


def scatter_about(own_key, dims, width, bound, cuts=(), kind=jnp.bfloat16):
    gain = shard_levels(own_key, dims, cuts, -0.22, 0.18) if cuts else 1.0
    drawn = jax.random.normal(own_key, dims, jnp.float32) * width * gain
    return jnp.minimum(jnp.maximum(drawn, -bound), bound).astype(kind)


def setup_inputs(seed: int = 0) -> dict:
    keys = jax.random.split(jax.random.key(seed), 4)
    raster = scatter_about(keys[0], (DIES, H, W), 2.0, 12.0, ((0, 2), (1, 4), (2, 4)), jnp.float32)
    shift_pick = touch_ends(jax.random.randint(keys[1], (DIES, TILE_ROWS, TILE_COLS), 0, 8), jax.random.fold_in(keys[1], 1), 0, 7).astype(jnp.int32)
    offsets = touch_ends(jax.random.randint(keys[2], (DIES, TILE_ROWS, TILE_COLS, 2), -R - 1, R + 1), jax.random.fold_in(keys[2], 1), -R - 1, R).astype(jnp.int32)
    return dict(raster=raster, shift_pick=shift_pick, offsets=offsets)


def gauss_taps(sigma):
    spots = jnp.arange(-RG, RG + 1).astype(jnp.float32)
    raw = jnp.exp(-spots * spots / (2.0 * sigma * sigma))
    return raw / jnp.sum(raw)


def blur_tile(image, sigma):
    taps = gauss_taps(sigma)
    column_sum = taps[0] * image[0:TH, :]
    for shift in range(1, 2 * RG + 1):
        column_sum = column_sum + taps[shift] * image[shift:shift + TH, :]
    total = taps[0] * column_sum[:, 0:TW]
    for shift in range(1, 2 * RG + 1):
        total = total + taps[shift] * column_sum[:, shift:shift + TW]
    return total


def tile_dog(block, row_off, col_off, pick):
    row_start = (row_off + R + 1).astype(jnp.int32)
    col_start = (col_off + R + 1).astype(jnp.int32)
    window = lax.dynamic_slice(block, (row_start, col_start), (TH + 2 * RG + 1, TW + 2 * RG + 1))
    frac_y = (pick % 4).astype(jnp.float32) * 0.25 + 0.125
    frac_x = (pick // 4).astype(jnp.float32) * 0.5 + 0.25
    upper = (1.0 - frac_x) * window[:-1, :-1] + frac_x * window[:-1, 1:]
    lower = (1.0 - frac_x) * window[1:, :-1] + frac_x * window[1:, 1:]
    aligned = (1.0 - frac_y) * upper + frac_y * lower
    return blur_tile(aligned, 1.0) - blur_tile(aligned, 2.0)


def reference(raster, shift_pick, offsets):
    padded = jnp.pad(raster, ((0, 0), (HW, HW), (HW, HW)))

    def one_tile(index):
        die_num = index // (TILE_ROWS * TILE_COLS)
        row_num = (index // TILE_COLS) % TILE_ROWS
        col_num = index % TILE_COLS
        block = lax.dynamic_slice(padded, (die_num, row_num * TH, col_num * TW), (1, TH + 2 * HW, TW + 2 * HW))[0]
        return tile_dog(block, offsets[die_num, row_num, col_num, 0], offsets[die_num, row_num, col_num, 1], shift_pick[die_num, row_num, col_num])

    indices = jnp.arange(DIES * TILE_ROWS * TILE_COLS, dtype=jnp.int32)
    dogs = lax.map(one_tile, indices)
    dogs = dogs.reshape(DIES, TILE_ROWS, TILE_COLS, TH, TW).transpose(0, 1, 3, 2, 4).reshape(DIES, H, W)
    change = dogs[1:] - dogs[:-1]
    zeros = jnp.zeros((1, H, W), dogs.dtype)
    next_map = jnp.concatenate([change, zeros], axis=0)
    prev_map = jnp.concatenate([zeros, change], axis=0)
    return next_map, prev_map
```

```python
import functools

import jax
import jax.numpy as jnp
import numpy as np
from jax import lax
from jax.experimental import pallas as pl
from jax.experimental.pallas import tpu as pltpu
from jax.sharding import PartitionSpec as P

TH = 256
TW = 1024
RG = 6
HW = 11
LANE = 128
FRAME = 16
STRIP = 2 * FRAME
MID = TH - 2 * FRAME
CORE = TW - 2 * LANE
WIDE = TW + LANE


def gauss_taps(sigma):
    spots = np.arange(-RG, RG + 1).astype(np.float64)
    raw = np.exp(-spots * spots / (2.0 * sigma * sigma))
    return [float(tap) for tap in np.float32(raw / raw.sum())[RG:]]


NARROW = gauss_taps(1.0)
BROAD = gauss_taps(2.0)


def split(values):
    high = values.astype(jnp.bfloat16)
    low = (values - high.astype(jnp.float32)).astype(jnp.bfloat16)
    return high, low


def bands(distance, frac):
    def look(spots):
        away = jnp.abs(spots)
        narrow = jnp.zeros(spots.shape, jnp.float32)
        broad = jnp.zeros(spots.shape, jnp.float32)
        for tap in range(RG + 1):
            here = away == tap
            narrow = jnp.where(here, NARROW[tap], narrow)
            broad = jnp.where(here, BROAD[tap], broad)
        return narrow, broad

    near = look(distance)
    far = look(distance - 1)
    return tuple((1.0 - frac) * a + frac * b for a, b in zip(near, far))


def column_weights(off_ref, pick_ref):
    frac = (pick_ref[0, 0, 0] // 4).astype(jnp.float32) * 0.5 + 0.25
    shape = (2 * LANE, LANE)
    distance = (
        lax.broadcasted_iota(jnp.int32, shape, 0)
        - lax.broadcasted_iota(jnp.int32, shape, 1)
        - (HW + off_ref[0, 0, 0, 1])
    )
    narrow, broad = bands(distance, frac)
    return split(jnp.concatenate([narrow, narrow - broad], axis=1))


def row_weights(off_ref, pick_ref, rows, depth, first):
    frac = (pick_ref[0, 0, 0] % 4).astype(jnp.float32) * 0.25 + 0.125
    shape = (rows, depth)
    distance = (
        lax.broadcasted_iota(jnp.int32, shape, 1)
        - lax.broadcasted_iota(jnp.int32, shape, 0)
        - (first + off_ref[0, 0, 0, 0])
    )
    narrow, broad = bands(distance, frac)
    return split(jnp.concatenate([narrow - broad, broad], axis=1))


def product(left, right):
    dot = functools.partial(jnp.dot, preferred_element_type=jnp.float32)
    return dot(left[0], right[0]) + (dot(left[1], right[0]) + dot(left[0], right[1]))


def core_kernel(off_ref, pick_ref, x_hbm, core_ref, first_ref, last_ref, x, xh, xl, th, tl, sem):
    halves = [pl.ds(0, LANE), pl.ds(LANE, LANE)]
    copies = [
        pltpu.make_async_copy(x_hbm.at[0, rows], x.at[rows], sem.at[k])
        for k, rows in enumerate(halves)
    ]
    for copy in copies:
        copy.start()
    column = column_weights(off_ref, pick_ref)
    row = row_weights(off_ref, pick_ref, MID, TH, FRAME)
    for half, (rows, copy) in enumerate(zip(halves, copies)):
        copy.wait()
        values = x[rows, :]
        first_ref[rows, :] = values[:, :LANE]
        last_ref[rows, :] = values[:, TW - LANE :]
        high, low = split(pltpu.roll(values, HW, 1))
        xh[rows, :] = high
        xl[rows, :] = low
        for block in range(CORE // LANE):
            window = pl.ds((block + 1) * LANE, 2 * LANE)
            summed = product((xh[rows, window], xl[rows, window]), column)
            high, low = split(summed)
            spot = pl.ds(block * LANE, LANE)
            for part in range(2):
                to = pl.ds(part * TH + half * LANE, LANE)
                th[to, spot] = high[:, part * LANE : (part + 1) * LANE]
                tl[to, spot] = low[:, part * LANE : (part + 1) * LANE]
    for block in range(CORE // (2 * LANE)):
        spot = pl.ds(block * 2 * LANE, 2 * LANE)
        core_ref[:, spot] = product(row, (th[:, spot], tl[:, spot]))


def side_kernel(off_ref, pick_ref, xl_ref, xr_ref, x_hbm, left_ref, right_ref, side_ref, head_ref, foot_ref, up_ref, down_ref, sem):
    copies = [
        pltpu.make_async_copy(x_hbm.at[0, pl.ds(0, STRIP)], head_ref.at[:, pl.ds(0, TW)], sem.at[0]),
        pltpu.make_async_copy(x_hbm.at[0, pl.ds(TH - STRIP, STRIP)], foot_ref.at[:, pl.ds(0, TW)], sem.at[1]),
        pltpu.make_async_copy(x_hbm.at[0, pl.ds(0, FRAME)], up_ref.at[:, pl.ds(0, TW)], sem.at[2]),
        pltpu.make_async_copy(x_hbm.at[0, pl.ds(TH - FRAME, FRAME)], down_ref.at[:, pl.ds(0, TW)], sem.at[3]),
    ]
    for copy in copies:
        copy.start()
    left = left_ref[...]
    right = right_ref[...]
    column = column_weights(off_ref, pick_ref)
    row = row_weights(off_ref, pick_ref, MID, TH, FRAME)
    pieces = []
    for strip in (
        jnp.concatenate([left, xl_ref[0]], axis=1),
        jnp.concatenate([xr_ref[0], right], axis=1),
    ):
        window = pltpu.roll(strip, 2 * LANE + HW, 1)[:, : 2 * LANE]
        summed = product(split(window), column)
        pieces.append(jnp.concatenate([summed[:, :LANE], summed[:, LANE:]], axis=0))
    side_ref[...] = product(row, split(jnp.concatenate(pieces, axis=1)))
    lane = lax.broadcasted_iota(jnp.int32, (TH, LANE), 1)
    edge = jnp.where(lane < LANE // 2, right, left)
    spot = pl.ds(TW, LANE)
    head_ref[:, spot] = edge[:STRIP]
    foot_ref[:, spot] = edge[TH - STRIP :]
    up_ref[:, spot] = edge[:FRAME]
    down_ref[:, spot] = edge[TH - FRAME :]
    for copy in copies:
        copy.wait()


def frame_kernel(off_ref, pick_ref, head_ref, foot_ref, top_ref, bottom_ref, frame_ref):
    column = column_weights(off_ref, pick_ref)
    depth = STRIP + FRAME
    row = row_weights(off_ref, pick_ref, FRAME, depth, FRAME)
    values = jnp.concatenate([top_ref[...], head_ref[...], foot_ref[...], bottom_ref[...]], axis=0)
    high, low = split(pltpu.roll(values, HW, 1))
    for pair in range(TW // (2 * LANE)):
        sums = []
        for block in (2 * pair, 2 * pair + 1):
            window = slice(block * LANE, (block + 2) * LANE)
            sums.append(product((high[:, window], low[:, window]), column))
        spot = pl.ds(pair * 2 * LANE, 2 * LANE)
        for end in range(2):
            rows = slice(end * depth, (end + 1) * depth)
            stacked = jnp.concatenate(
                [
                    jnp.concatenate([s[rows, :LANE] for s in sums], axis=1),
                    jnp.concatenate([s[rows, LANE:] for s in sums], axis=1),
                ],
                axis=0,
            )
            frame_ref[pl.ds(end * FRAME, FRAME), spot] = product(row, split(stacked))


SMALL = pl.BlockSpec(memory_space=pltpu.SMEM)
FAST = pl.BlockSpec(memory_space=pltpu.VMEM)
ANY = pl.BlockSpec(memory_space=pl.ANY)
LIMIT = pltpu.CompilerParams(vmem_limit_bytes=16 * 2**20)


def f32(*shape):
    return jax.ShapeDtypeStruct(shape, jnp.float32)


def core_call(offsets, pick, raster):
    wide = pltpu.VMEM((TH, TW), jnp.bfloat16)
    tall = pltpu.VMEM((2 * TH, CORE), jnp.bfloat16)
    return pl.pallas_call(
        core_kernel,
        out_shape=(f32(MID, CORE), f32(TH, LANE), f32(TH, LANE)),
        in_specs=[SMALL, SMALL, ANY],
        out_specs=(FAST, FAST, FAST),
        scratch_shapes=[
            pltpu.VMEM((TH, TW), jnp.float32), wide, wide, tall, tall, pltpu.SemaphoreType.DMA((2,)),
        ],
        compiler_params=LIMIT,
        cost_estimate=pl.CostEstimate(flops=2 * 10**9, bytes_accessed=3 * 2**20, transcendentals=0),
        name="core",
    )(offsets, pick, raster)


def side_call(offsets, pick, raster, left, right):
    ends = [
        pl.BlockSpec((1, TH, 2 * LANE), lambda step: (0, 0, 0)),
        pl.BlockSpec((1, TH, 2 * LANE), lambda step: (0, 0, TW // (2 * LANE) - 1)),
    ]
    return pl.pallas_call(
        side_kernel,
        grid=(1,),
        out_shape=(f32(MID, 2 * LANE), f32(STRIP, WIDE), f32(STRIP, WIDE), f32(FRAME, WIDE), f32(FRAME, WIDE)),
        in_specs=[SMALL, SMALL, *ends, ANY, FAST, FAST],
        out_specs=(FAST,) * 5,
        scratch_shapes=[pltpu.SemaphoreType.DMA((4,))],
        compiler_params=LIMIT,
        cost_estimate=pl.CostEstimate(flops=10**9, bytes_accessed=2**20, transcendentals=0),
        name="side",
    )(offsets, pick, raster, raster, raster, left, right)


def frame_call(offsets, pick, head, foot, top, bottom):
    return pl.pallas_call(
        frame_kernel,
        out_shape=f32(2 * FRAME, TW),
        in_specs=[SMALL, SMALL, FAST, FAST, FAST, FAST],
        out_specs=FAST,
        compiler_params=LIMIT,
        cost_estimate=pl.CostEstimate(flops=10**9, bytes_accessed=2**20, transcendentals=0),
        name="frame",
    )(offsets, pick, head, foot, top, bottom)


def change_kernel(places, count, own_ref, *refs):
    next_out, prev_out, later, earlier, sem = refs[-5:]
    others = refs[: 1 if count == 2 else 2]
    position = lax.axis_index("die")
    own = own_ref[...]
    later[...] = jnp.where(position < count - 1, others[0][...] - own, 0.0)
    earlier[...] = jnp.where(position > 0, own - others[-1][...], 0.0)
    copies = []
    for source, target in places:
        for values, out in ((later, next_out), (earlier, prev_out)):
            spot = sem.at[len(copies)]
            copies.append(pltpu.make_async_copy(values.at[source], out.at[(0, *target)], spot))
    for copy in copies:
        copy.start()
    for copy in copies:
        copy.wait()


def change_call(count, places, own, others, maps):
    out = f32(1, TH, TW)
    first = 1 + len(others)
    return pl.pallas_call(
        functools.partial(change_kernel, places, count),
        out_shape=(out, out),
        in_specs=[FAST] * first + [ANY] * len(maps),
        out_specs=(ANY, ANY),
        scratch_shapes=[
            pltpu.VMEM(own.shape, jnp.float32),
            pltpu.VMEM(own.shape, jnp.float32),
            pltpu.SemaphoreType.DMA((2 * len(places),)),
        ],
        input_output_aliases={first + k: k for k in range(len(maps))},
        compiler_params=LIMIT,
        cost_estimate=pl.CostEstimate(flops=2 * own.size, bytes_accessed=20 * own.size, transcendentals=0),
        name="change",
    )(own, *others, *maps)


ALL = pl.ds(0, MID)
ROWS = pl.ds(FRAME, MID)
CORE_PLACES = (((ALL, pl.ds(0, CORE)), (ROWS, pl.ds(LANE, CORE))),)
SIDE_PLACES = (
    ((ALL, pl.ds(0, LANE)), (ROWS, pl.ds(0, LANE))),
    ((ALL, pl.ds(LANE, LANE)), (ROWS, pl.ds(TW - LANE, LANE))),
)
FRAME_PLACES = (
    ((pl.ds(0, FRAME), pl.ds(0, TW)), (pl.ds(0, FRAME), pl.ds(0, TW))),
    ((pl.ds(FRAME, FRAME), pl.ds(0, TW)), (pl.ds(TH - FRAME, FRAME), pl.ds(0, TW))),
)


def from_before(block, axis):
    return lax.ppermute(block, axis, [(i, i + 1) for i in range(lax.axis_size(axis) - 1)])


def from_after(block, axis):
    return lax.ppermute(block, axis, [(i + 1, i) for i in range(lax.axis_size(axis) - 1)])


def other_dies(block):
    if lax.axis_size("die") == 2:
        return (lax.ppermute(block, "die", [(0, 1), (1, 0)]),)
    return (from_after(block, "die"), from_before(block, "die"))


def body(raster, shift_pick, offsets):
    count = lax.axis_size("die")
    core, first, last = core_call(offsets, shift_pick, raster)
    core_others = other_dies(core)
    left = from_before(last, "tx")
    right = from_after(first, "tx")
    side, head, foot, up, down = side_call(offsets, shift_pick, raster, left, right)
    side_others = other_dies(side)
    top = from_before(down, "ty")
    bottom = from_after(up, "ty")
    frame = frame_call(offsets, shift_pick, head, foot, top, bottom)
    frame_others = other_dies(frame)
    maps = change_call(count, CORE_PLACES, core, core_others, ())
    maps = change_call(count, SIDE_PLACES, side, side_others, maps)
    return tuple(change_call(count, FRAME_PLACES, frame, frame_others, maps))


def solution(mesh):
    in_specs = (P("die", "ty", "tx"), P("die", "ty", "tx"), P("die", "ty", "tx", None))
    out_specs = (P("die", "ty", "tx"), P("die", "ty", "tx"))
    return jax.shard_map(body, mesh=mesh, in_specs=in_specs, out_specs=out_specs, check_vma=False)
```

```python
import functools

import jax
import jax.numpy as jnp
import numpy as np
from jax import lax
from jax.experimental import pallas as pl
from jax.experimental.pallas import tpu as pltpu
from jax.sharding import PartitionSpec as P

TH = 256
TW = 1024
RG = 6
HW = 11
LANE = 128
FRAME = 16
STRIP = 2 * FRAME
CORE = TW - 2 * LANE
LEAD = 96
DEPTH = LEAD + 2 * FRAME
MID = TH - 2 * FRAME
REST = MID - LEAD
BF16 = jnp.bfloat16


def gauss_taps(sigma):
    spots = np.arange(-RG, RG + 1).astype(np.float64)
    raw = np.exp(-spots * spots / (2.0 * sigma * sigma))
    return [float(tap) for tap in np.float32(raw / raw.sum())[RG:]]


NARROW = gauss_taps(1.0)
BROAD = gauss_taps(2.0)


def split(values):
    high = values.astype(BF16)
    low = (values - high.astype(jnp.float32)).astype(BF16)
    return high, low


def bands(distance, frac):
    def look(spots):
        away = jnp.abs(spots)
        narrow = jnp.zeros(spots.shape, jnp.float32)
        broad = jnp.zeros(spots.shape, jnp.float32)
        for tap in range(RG + 1):
            here = away == tap
            narrow = jnp.where(here, NARROW[tap], narrow)
            broad = jnp.where(here, BROAD[tap], broad)
        return narrow, broad

    near = look(distance)
    far = look(distance - 1)
    return tuple((1.0 - frac) * a + frac * b for a, b in zip(near, far))


def column_weights(offset, pick):
    frac = (pick // 4).astype(jnp.float32) * 0.5 + 0.25
    shape = (2 * LANE, LANE)
    window = lax.broadcasted_iota(jnp.int32, shape, 0)
    result = lax.broadcasted_iota(jnp.int32, shape, 1)
    narrow, broad = bands(window - result - (HW + offset), frac)
    return split(jnp.concatenate([narrow, narrow - broad], axis=1))


def row_weights(offset, pick):
    frac = (pick % 4).astype(jnp.float32) * 0.25 + 0.125
    shape = (LEAD, DEPTH)
    source = lax.broadcasted_iota(jnp.int32, shape, 1)
    result = lax.broadcasted_iota(jnp.int32, shape, 0)
    narrow, broad = bands(source - result - (FRAME + offset), frac)
    return split(jnp.concatenate([narrow - broad, broad], axis=1))


def product(left, right):
    dot = functools.partial(jnp.dot, preferred_element_type=jnp.float32)
    return dot(left[0], right[0]) + (dot(left[1], right[0]) + dot(left[0], right[1]))


def column_sums(windows, column):
    rows = windows[0].shape[0]
    sums = split(product(split(jnp.concatenate(windows, axis=0)), column))
    blocks = [slice(k * rows, (k + 1) * rows) for k in range(len(windows))]
    return [
        [jnp.concatenate([half[block, part] for block in blocks], axis=1) for half in sums]
        for part in (slice(0, LANE), slice(LANE, 2 * LANE))
    ]


def row_sums(row, sums, rows):
    narrow, change = sums
    stacked = [jnp.concatenate([a[rows], b[rows]], axis=0) for a, b in zip(narrow, change)]
    return product(row, stacked)


def core_windows(values):
    rolled = pltpu.roll(values, HW, 1)
    return [rolled[:, block * LANE : (block + 2) * LANE] for block in range(1, TW // LANE - 1)]


def lead_kernel(off_hbm, pick_hbm, x_hbm, lead, first, second, wh, wl, vh, vl, x, off, pick, sem):
    odd = lax.axis_index("tx") % 2
    spots = [pl.multiple_of(LANE * (TW // LANE - 1) * side, LANE) for side in (1 - odd, odd)]
    copies = [
        pltpu.make_async_copy(off_hbm, off, sem.at[0]),
        pltpu.make_async_copy(pick_hbm, pick, sem.at[1]),
        pltpu.make_async_copy(x_hbm.at[0, pl.ds(0, DEPTH)], x, sem.at[2]),
        pltpu.make_async_copy(x_hbm.at[0, :, pl.ds(spots[0], LANE)], first, sem.at[3]),
        pltpu.make_async_copy(x_hbm.at[0, :, pl.ds(spots[1], LANE)], second, sem.at[4]),
    ]
    for copy in copies:
        copy.start()
    copies[0].wait()
    copies[1].wait()
    column = column_weights(off[0, 0, 0, 1], pick[0, 0, 0])
    row = row_weights(off[0, 0, 0, 0], pick[0, 0, 0])
    wh[...], wl[...] = column
    vh[...], vl[...] = row
    copies[2].wait()
    sums = column_sums(core_windows(x[...]), column)
    lead[...] = row_sums(row, sums, slice(0, DEPTH))
    copies[3].wait()
    copies[4].wait()


def rest_kernel(x, wh, wl, vh, vl, rest):
    column = (wh[...], wl[...])
    row = (vh[...], vl[...])
    sums = column_sums(core_windows(x[0, LEAD:, :]), column)
    rest[:LEAD, :] = row_sums(row, sums, slice(0, DEPTH))
    last = REST - LEAD
    lower = [v[LEAD - last :] for v in row]
    rest[LEAD:, :] = row_sums(lower, sums, slice(TH - LEAD - DEPTH, TH - LEAD))


def halos(axis, first, second):
    place = lax.axis_index(axis)
    inner = (place > 0) & (place < lax.axis_size(axis) - 1)
    even = place % 2 == 0
    second = jnp.where(inner, second, 0.0)
    return jnp.where(even, second, first), jnp.where(even, first, second)


def edge_block(before, after):
    lane = lax.broadcasted_iota(jnp.int32, before.shape, 1)
    return jnp.where(lane < LANE // 2, after, before)


def side_kernel(x, first, second, wh, wl, vh, vl, side, send_first, send_second):
    column = (wh[...], wl[...])
    row = (vh[...], vl[...])
    before, after = halos("tx", first[...], second[...])
    windows = [
        pltpu.roll(jnp.concatenate(strip, axis=1), 2 * LANE + HW, 1)[:, : 2 * LANE]
        for strip in ((before, x[0, :, : 2 * LANE]), (x[0, :, TW - 2 * LANE :], after))
    ]
    sums = column_sums(windows, column)
    side[:LEAD, :] = row_sums(row, sums, slice(0, DEPTH))
    side[LEAD : 2 * LEAD, :] = row_sums(row, sums, slice(LEAD, LEAD + DEPTH))
    last = MID - 2 * LEAD
    lower = [v[LEAD - last :] for v in row]
    side[2 * LEAD :, :] = row_sums(lower, sums, slice(TH - DEPTH, TH))
    edge = edge_block(before, after)
    top = jnp.concatenate([x[0, :FRAME, :], edge[:FRAME]], axis=1)
    bottom = jnp.concatenate([x[0, TH - FRAME :, :], edge[TH - FRAME :]], axis=1)
    even = lax.axis_index("ty") % 2 == 0
    send_first[...] = jnp.where(even, bottom, top)
    send_second[...] = jnp.where(even, top, bottom)


def frame_kernel(x, first, second, row_first, row_second, wh, wl, vh, vl, frame):
    column = (wh[...], wl[...])
    top, bottom = halos("ty", row_first[...], row_second[...])
    own = []
    for rows in (slice(0, STRIP), slice(TH - STRIP, TH)):
        edge = edge_block(*halos("tx", first[rows, :], second[rows, :]))
        own.append(jnp.concatenate([x[0, rows, :], edge], axis=1))
    values = jnp.concatenate([top, own[0], own[1], bottom], axis=0)
    rolled = pltpu.roll(values, HW, 1)
    windows = [rolled[:, block * LANE : (block + 2) * LANE] for block in range(TW // LANE)]
    sums = column_sums(windows, column)
    tall = values.shape[0]
    filler = jnp.zeros((DEPTH - tall, TW), BF16)
    padded = [[jnp.concatenate([half, filler], axis=0) for half in part] for part in sums]
    row = [jnp.concatenate([v[:FRAME, :], v[tall // 2 : tall // 2 + FRAME, :]], axis=0) for v in (vh, vl)]
    frame[...] = row_sums(row, padded, slice(0, DEPTH))


FAST = pl.BlockSpec(memory_space=pltpu.VMEM)
SLOW = pl.BlockSpec(memory_space=pltpu.HBM)
ANY = pl.BlockSpec(memory_space=pl.ANY)
LIMIT = pltpu.CompilerParams(vmem_limit_bytes=16 * 2**20)


def f32(*shape):
    return jax.ShapeDtypeStruct(shape, jnp.float32)


def bf16(*shape):
    return jax.ShapeDtypeStruct(shape, BF16)


def cost(flops):
    return pl.CostEstimate(flops=flops, bytes_accessed=2**12, transcendentals=0)


def lead_call(offsets, pick, raster):
    column = bf16(2 * LANE, 2 * LANE)
    row = bf16(LEAD, 2 * DEPTH)
    return pl.pallas_call(
        lead_kernel,
        out_shape=(f32(LEAD, CORE), f32(TH, LANE), f32(TH, LANE), column, column, row, row),
        in_specs=[SLOW] * 3,
        out_specs=(FAST,) * 7,
        scratch_shapes=[
            pltpu.VMEM((DEPTH, TW), jnp.float32),
            pltpu.SMEM(offsets.shape, jnp.int32),
            pltpu.SMEM(pick.shape, jnp.int32),
            pltpu.SemaphoreType.DMA((5,)),
        ],
        compiler_params=LIMIT,
        cost_estimate=cost(10**6),
        name="lead",
    )(offsets, pick, pltpu.with_memory_space_constraint(raster, pltpu.HBM))


def fast_call(kernel, name, out_shape, *operands):
    many = isinstance(out_shape, tuple)
    return pl.pallas_call(
        kernel,
        out_shape=out_shape,
        in_specs=[FAST] * len(operands),
        out_specs=(FAST,) * len(out_shape) if many else FAST,
        compiler_params=LIMIT,
        cost_estimate=cost(10**6),
        name=name,
    )(*operands)


def change_kernel(blocks, count, fill, *refs):
    width = 2 if count == 2 else 3
    pieces = [refs[k * width : (k + 1) * width] for k in range(len(blocks))]
    scratch = len(blocks) + 1 + bool(fill)
    outs = refs[-scratch - 2 : -scratch]
    values = refs[-scratch:][: len(blocks)]
    sem = refs[-1]
    position = lax.axis_index("die")
    for out, there, forward in (
        (outs[0], position < count - 1, True),
        (outs[1], position > 0, False),
    ):

        @pl.when(there)
        def _():
            copies = []
            for piece, value, places in zip(pieces, values, blocks):
                own = piece[0][...]
                value[...] = piece[1][...] - own if forward else own - piece[-1][...]
                for (row, column), (out_row, out_column), (tall, wide) in places:
                    copies.append(
                        pltpu.make_async_copy(
                            value.at[pl.ds(row, tall), pl.ds(column, wide)],
                            out.at[0, pl.ds(out_row, tall), pl.ds(out_column, wide)],
                            sem.at[len(copies)],
                        )
                    )
                    copies[-1].start()
            for copy in copies:
                copy.wait()

        if fill:

            @pl.when(jnp.logical_not(there))
            def _():
                zeros = refs[-2]
                zeros[...] = jnp.zeros_like(zeros)
                copy = pltpu.make_async_copy(zeros, out.at[0], sem.at[0])
                copy.start()
                copy.wait()


def change_call(count, blocks, pieces, maps):
    operands = [array for own, others in pieces for array in (own, *others)]
    fill = not maps
    out = f32(1, TH, TW)
    return pl.pallas_call(
        functools.partial(change_kernel, blocks, count, fill),
        out_shape=(out, out),
        in_specs=[FAST] * len(operands) + [SLOW] * len(maps),
        out_specs=(SLOW, SLOW),
        scratch_shapes=[
            *(pltpu.VMEM(own.shape, jnp.float32) for own, _ in pieces),
            *([pltpu.VMEM((TH, TW), jnp.float32)] if fill else []),
            pltpu.SemaphoreType.DMA((sum(map(len, blocks)),)),
        ],
        input_output_aliases={len(operands) + k: k for k in range(len(maps))},
        compiler_params=LIMIT,
        cost_estimate=cost(10**6),
        name="change",
    )(*operands, *maps)


CORE_PLACES = (
    (((0, 0), (FRAME, LANE), (LEAD, CORE)),),
    (((0, 0), (FRAME + LEAD, LANE), (REST, CORE)),),
)
SIDE_PLACES = ((((0, 0), (FRAME, 0), (MID, LANE)), ((0, LANE), (FRAME, TW - LANE), (MID, LANE))),)
FRAME_PLACES = ((((0, 0), (0, 0), (FRAME, TW)), ((FRAME, 0), (TH - FRAME, 0), (FRAME, TW))),)


def swap_rounds(axis, first, second):
    count = lax.axis_size(axis)
    assert count % 2 == 0
    pairs = [(i, i ^ 1) for i in range(count)]
    others = [(i, min(max((i ^ 1) + 2 * (i % 2 * 2 - 1), 0), count - 1)) for i in range(count)]
    return lax.ppermute(first, axis, pairs), lax.ppermute(second, axis, others)


def other_dies(block):
    count = lax.axis_size("die")
    forward = [(i, i + 1) for i in range(count - 1)]
    backward = [(i + 1, i) for i in range(count - 1)]
    if count == 2:
        return (lax.ppermute(block, "die", forward + backward),)
    return (lax.ppermute(block, "die", backward), lax.ppermute(block, "die", forward))


def body(raster, shift_pick, offsets):
    count = lax.axis_size("die")
    lead, first, second, *weights = lead_call(offsets, shift_pick, raster)
    lead_others = other_dies(lead)
    first, second = swap_rounds("tx", first, second)
    rest = fast_call(rest_kernel, "rest", f32(REST, CORE), raster, *weights)
    rest_others = other_dies(rest)
    halo = f32(FRAME, TW + LANE)
    side, send_first, send_second = fast_call(
        side_kernel, "side", (f32(MID, 2 * LANE), halo, halo), raster, first, second, *weights
    )
    side_others = other_dies(side)
    row_first, row_second = swap_rounds("ty", send_first, send_second)
    frame = fast_call(
        frame_kernel, "frame", f32(STRIP, TW), raster, first, second, row_first, row_second, *weights
    )
    frame_others = other_dies(frame)
    maps = change_call(count, CORE_PLACES, [(lead, lead_others), (rest, rest_others)], ())
    maps = change_call(count, SIDE_PLACES, [(side, side_others)], maps)
    return tuple(change_call(count, FRAME_PLACES, [(frame, frame_others)], maps))


def solution(mesh):
    in_specs = (P("die", "ty", "tx"), P("die", "ty", "tx"), P("die", "ty", "tx", None))
    out_specs = (P("die", "ty", "tx"), P("die", "ty", "tx"))
    return jax.shard_map(body, mesh=mesh, in_specs=in_specs, out_specs=out_specs, check_vma=False)
```

```python
import functools

import jax
import jax.numpy as jnp
import numpy as np
from jax import lax
from jax.experimental import pallas as pl
from jax.experimental.pallas import tpu as pltpu
from jax.sharding import PartitionSpec as P

TH = 256
TW = 1024
RG = 6
HW = 11
LANE = 128
FRAME = 16
STRIP = 2 * FRAME
CORE = TW - 2 * LANE
SPAN = 96
DEPTH = SPAN + 2 * FRAME
MID = TH - 2 * FRAME
LEAD = 80
REST = MID - LEAD
REACH = LANE + 2 * FRAME
BF16 = jnp.bfloat16


def gauss_taps(sigma):
    spots = np.arange(-RG, RG + 1).astype(np.float64)
    raw = np.exp(-spots * spots / (2.0 * sigma * sigma))
    return [float(tap) for tap in np.float32(raw / raw.sum())[RG:]]


NARROW = gauss_taps(1.0)
BROAD = gauss_taps(2.0)


def split(values):
    high = values.astype(BF16)
    low = (values - high.astype(jnp.float32)).astype(BF16)
    return high, low


def bands(distance, frac):
    def look(spots):
        away = jnp.abs(spots)
        narrow = jnp.zeros(spots.shape, jnp.float32)
        broad = jnp.zeros(spots.shape, jnp.float32)
        for tap in range(RG + 1):
            here = away == tap
            narrow = jnp.where(here, NARROW[tap], narrow)
            broad = jnp.where(here, BROAD[tap], broad)
        return narrow, broad

    near = look(distance)
    far = look(distance - 1)
    return tuple((1.0 - frac) * a + frac * b for a, b in zip(near, far))


def column_weights(offset, pick):
    frac = (pick // 4).astype(jnp.float32) * 0.5 + 0.25
    shape = (REACH, LANE)
    window = lax.broadcasted_iota(jnp.int32, shape, 0)
    result = lax.broadcasted_iota(jnp.int32, shape, 1)
    narrow, broad = bands(window - result - (HW + offset), frac)
    weights = split(jnp.concatenate([narrow, narrow - broad], axis=1))
    zeros = jnp.zeros((2 * LANE - REACH, 2 * LANE), BF16)
    return tuple(jnp.concatenate([half, zeros], axis=0) for half in weights)


def row_weights(offset, pick):
    frac = (pick % 4).astype(jnp.float32) * 0.25 + 0.125
    shape = (SPAN, DEPTH)
    source = lax.broadcasted_iota(jnp.int32, shape, 1)
    result = lax.broadcasted_iota(jnp.int32, shape, 0)
    narrow, broad = bands(source - result - (FRAME + offset), frac)
    return split(jnp.concatenate([narrow - broad, broad], axis=1))


def product(left, right):
    dot = functools.partial(jnp.dot, preferred_element_type=jnp.float32)
    return dot(left[0], right[0]) + (dot(left[1], right[0]) + dot(left[0], right[1]))


def column_sums(windows, column):
    rows = windows[0].shape[0]
    sums = split(product(split(jnp.concatenate(windows, axis=0)), column))
    blocks = [slice(k * rows, (k + 1) * rows) for k in range(len(windows))]
    return [
        [jnp.concatenate([half[block, part] for block in blocks], axis=1) for half in sums]
        for part in (slice(0, LANE), slice(LANE, 2 * LANE))
    ]


def row_sums(row, sums, first=0):
    narrow, change = sums
    short = DEPTH - (narrow[0].shape[0] - first)
    filler = [jnp.zeros((short, narrow[0].shape[1]), BF16)] if short > 0 else []
    rows = slice(first, first + DEPTH)
    stacked = [jnp.concatenate([a[rows], *filler, b[rows], *filler], axis=0) for a, b in zip(narrow, change)]
    return product(row, stacked)


def core_windows(values):
    rolled = pltpu.roll(values, HW, 1)
    return [rolled[:, block * LANE : (block + 2) * LANE] for block in range(1, TW // LANE - 1)]


def lead_kernel(off_hbm, pick_hbm, x_hbm, lead, first, second, wh, wl, vh, vl, x, off, pick, sem):
    odd = lax.axis_index("tx") % 2
    spots = [pl.multiple_of(LANE * (TW // LANE - 1) * side, LANE) for side in (1 - odd, odd)]
    copies = [
        pltpu.make_async_copy(off_hbm, off, sem.at[0]),
        pltpu.make_async_copy(pick_hbm, pick, sem.at[1]),
        pltpu.make_async_copy(x_hbm.at[0, pl.ds(0, LEAD + 2 * FRAME)], x, sem.at[2]),
        pltpu.make_async_copy(x_hbm.at[0, :, pl.ds(spots[0], LANE)], first, sem.at[3]),
        pltpu.make_async_copy(x_hbm.at[0, :, pl.ds(spots[1], LANE)], second, sem.at[4]),
    ]
    for copy in copies:
        copy.start()
    copies[0].wait()
    copies[1].wait()
    column = column_weights(off[0, 0, 0, 1], pick[0, 0, 0])
    row = row_weights(off[0, 0, 0, 0], pick[0, 0, 0])
    wh[...], wl[...] = column
    vh[...], vl[...] = row
    copies[2].wait()
    sums = column_sums(core_windows(x[...]), column)
    lead[...] = row_sums([half[:LEAD] for half in row], sums)
    copies[3].wait()
    copies[4].wait()


def rest_kernel(x, wh, wl, vh, vl, rest):
    column = (wh[...], wl[...])
    row = (vh[...], vl[...])
    sums = column_sums(core_windows(x[0, LEAD:, :]), column)
    rest[:SPAN, :] = row_sums(row, sums)
    last = REST - SPAN
    lower = [half[SPAN - last :] for half in row]
    rest[SPAN:, :] = row_sums(lower, sums, TH - DEPTH - LEAD)


def halos(axis, first, second):
    place = lax.axis_index(axis)
    inner = (place > 0) & (place < lax.axis_size(axis) - 1)
    even = place % 2 == 0
    second = jnp.where(inner, second, 0.0)
    return jnp.where(even, second, first), jnp.where(even, first, second)


def edge_block(before, after):
    lane = lax.broadcasted_iota(jnp.int32, before.shape, 1)
    return jnp.where(lane < LANE // 2, after, before)


def side_kernel(x, first, second, wh, wl, vh, vl, side, send_first, send_second):
    column = (wh[...], wl[...])
    row = (vh[...], vl[...])
    before, after = halos("tx", first[...], second[...])
    windows = [
        pltpu.roll(jnp.concatenate(strip, axis=1), 2 * LANE + HW, 1)[:, : 2 * LANE]
        for strip in ((before, x[0, :, : 2 * LANE]), (x[0, :, TW - 2 * LANE :], after))
    ]
    sums = column_sums(windows, column)
    side[:SPAN, :] = row_sums(row, sums)
    side[SPAN : 2 * SPAN, :] = row_sums(row, sums, SPAN)
    last = MID - 2 * SPAN
    lower = [half[SPAN - last :] for half in row]
    side[2 * SPAN :, :] = row_sums(lower, sums, TH - DEPTH)
    edge = edge_block(before, after)
    top = jnp.concatenate([x[0, :FRAME, :], edge[:FRAME]], axis=1)
    bottom = jnp.concatenate([x[0, TH - FRAME :, :], edge[TH - FRAME :]], axis=1)
    even = lax.axis_index("ty") % 2 == 0
    send_first[...] = jnp.where(even, bottom, top)
    send_second[...] = jnp.where(even, top, bottom)


def frame_kernel(x, first, second, row_first, row_second, wh, wl, vh, vl, frame):
    column = (wh[...], wl[...])
    top, bottom = halos("ty", row_first[...], row_second[...])
    own = []
    for rows in (slice(0, STRIP), slice(TH - STRIP, TH)):
        edge = edge_block(*halos("tx", first[rows, :], second[rows, :]))
        own.append(jnp.concatenate([x[0, rows, :], edge], axis=1))
    values = jnp.concatenate([top, own[0], own[1], bottom], axis=0)
    rolled = pltpu.roll(values, HW, 1)
    windows = [rolled[:, block * LANE : (block + 2) * LANE] for block in range(TW // LANE)]
    sums = column_sums(windows, column)
    below = values.shape[0] // 2
    row = [jnp.concatenate([half[:FRAME, :], half[below : below + FRAME, :]], axis=0) for half in (vh, vl)]
    frame[...] = row_sums(row, sums)


CHANGE_COST = 10**10
FAST = pl.BlockSpec(memory_space=pltpu.VMEM)
SLOW = pl.BlockSpec(memory_space=pltpu.HBM)
LIMIT = pltpu.CompilerParams(vmem_limit_bytes=16 * 2**20)


def f32(*shape):
    return jax.ShapeDtypeStruct(shape, jnp.float32)


def bf16(*shape):
    return jax.ShapeDtypeStruct(shape, BF16)


def cost(flops):
    return pl.CostEstimate(flops=flops, bytes_accessed=2**12, transcendentals=0)


def keep(array):
    return pltpu.with_memory_space_constraint(array, pltpu.HBM)


def lead_call(offsets, pick, raster):
    column = bf16(2 * LANE, 2 * LANE)
    row = bf16(SPAN, 2 * DEPTH)
    return pl.pallas_call(
        lead_kernel,
        out_shape=(f32(LEAD, CORE), f32(TH, LANE), f32(TH, LANE), column, column, row, row),
        in_specs=[SLOW] * 3,
        out_specs=(FAST,) * 7,
        scratch_shapes=[
            pltpu.VMEM((LEAD + 2 * FRAME, TW), jnp.float32),
            pltpu.SMEM(offsets.shape, jnp.int32),
            pltpu.SMEM(pick.shape, jnp.int32),
            pltpu.SemaphoreType.DMA((5,)),
        ],
        compiler_params=LIMIT,
        cost_estimate=cost(10**6),
        name="lead",
    )(keep(offsets), pick, keep(raster))


def fast_call(kernel, name, out_shape, *operands):
    many = isinstance(out_shape, tuple)
    return pl.pallas_call(
        kernel,
        out_shape=out_shape,
        in_specs=[FAST] * len(operands),
        out_specs=(FAST,) * len(out_shape) if many else FAST,
        compiler_params=LIMIT,
        cost_estimate=cost(10**6),
        name=name,
    )(*operands)


def change_kernel(places, count, fill, own_ref, *refs):
    others = refs[: 1 if count == 2 else 2]
    next_out, prev_out, value = refs[-4 - fill :][:3]
    sem = refs[-1]
    position = lax.axis_index("die")
    for out, there, forward in (
        (next_out, position < count - 1, True),
        (prev_out, position > 0, False),
    ):

        @pl.when(there)
        def _():
            own = own_ref[...]
            value[...] = others[0][...] - own if forward else own - others[-1][...]
            copies = [
                pltpu.make_async_copy(
                    value.at[pl.ds(row, tall), pl.ds(column, wide)],
                    out.at[0, pl.ds(out_row, tall), pl.ds(out_column, wide)],
                    sem.at[k],
                )
                for k, ((row, column), (out_row, out_column), (tall, wide)) in enumerate(places)
            ]
            for copy in copies:
                copy.start()
            for copy in copies:
                copy.wait()

        if fill:

            @pl.when(jnp.logical_not(there))
            def _():
                zeros = refs[-2]
                zeros[...] = jnp.zeros_like(zeros)
                copy = pltpu.make_async_copy(zeros, out.at[0], sem.at[0])
                copy.start()
                copy.wait()


def change_call(count, places, own, others, maps):
    operands = (own, *others)
    fill = not maps
    out = f32(1, TH, TW)
    return pl.pallas_call(
        functools.partial(change_kernel, places, count, fill),
        out_shape=(out, out),
        in_specs=[FAST] * len(operands) + [SLOW] * len(maps),
        out_specs=(SLOW, SLOW),
        scratch_shapes=[
            pltpu.VMEM(own.shape, jnp.float32),
            *([pltpu.VMEM((TH, TW), jnp.float32)] if fill else []),
            pltpu.SemaphoreType.DMA((len(places),)),
        ],
        input_output_aliases={len(operands) + k: k for k in range(len(maps))},
        compiler_params=LIMIT,
        cost_estimate=cost(CHANGE_COST),
        name="change",
    )(*operands, *maps)


LEAD_PLACES = (((0, 0), (FRAME, LANE), (LEAD, CORE)),)
REST_PLACES = (((0, 0), (FRAME + LEAD, LANE), (REST, CORE)),)
SIDE_PLACES = (((0, 0), (FRAME, 0), (MID, LANE)), ((0, LANE), (FRAME, TW - LANE), (MID, LANE)))
FRAME_PLACES = (((0, 0), (0, 0), (FRAME, TW)), ((FRAME, 0), (TH - FRAME, 0), (FRAME, TW)))


def swap_rounds(axis, first, second):
    count = lax.axis_size(axis)
    assert count % 2 == 0
    pairs = [(i, i ^ 1) for i in range(count)]
    others = [(i, min(max((i ^ 1) + 2 * (i % 2 * 2 - 1), 0), count - 1)) for i in range(count)]
    return lax.ppermute(first, axis, pairs), lax.ppermute(second, axis, others)


def other_dies(block):
    count = lax.axis_size("die")
    forward = [(i, i + 1) for i in range(count - 1)]
    backward = [(i + 1, i) for i in range(count - 1)]
    if count == 2:
        return (lax.ppermute(block, "die", forward + backward),)
    return (lax.ppermute(block, "die", backward), lax.ppermute(block, "die", forward))


def body(raster, shift_pick, offsets):
    count = lax.axis_size("die")
    lead, first, second, *weights = lead_call(offsets, shift_pick, raster)
    lead_others = other_dies(lead)
    first, second = swap_rounds("tx", first, second)
    rest = fast_call(rest_kernel, "rest", f32(REST, CORE), raster, *weights)
    rest_others = other_dies(rest)
    halo = f32(FRAME, TW + LANE)
    side, send_first, send_second = fast_call(
        side_kernel, "side", (f32(MID, 2 * LANE), halo, halo), raster, first, second, *weights
    )
    side_others = other_dies(side)
    row_first, row_second = swap_rounds("ty", send_first, send_second)
    frame = fast_call(
        frame_kernel, "frame", f32(STRIP, TW), raster, first, second, row_first, row_second, *weights
    )
    frame_others = other_dies(frame)
    maps = change_call(count, LEAD_PLACES, lead, lead_others, ())
    maps = change_call(count, REST_PLACES, rest, rest_others, maps)
    maps = change_call(count, SIDE_PLACES, side, side_others, maps)
    return tuple(change_call(count, FRAME_PLACES, frame, frame_others, maps))


def solution(mesh):
    in_specs = (P("die", "ty", "tx"), P("die", "ty", "tx"), P("die", "ty", "tx", None))
    out_specs = (P("die", "ty", "tx"), P("die", "ty", "tx"))
    return jax.shard_map(body, mesh=mesh, in_specs=in_specs, out_specs=out_specs, check_vma=False)
```

```python
import functools

import jax
import jax.numpy as jnp
import numpy as np
from jax import lax
from jax.experimental import pallas as pl
from jax.experimental.pallas import tpu as pltpu
from jax.sharding import PartitionSpec as P

TH = 256
TW = 1024
RG = 6
HW = 11
LANE = 128
FRAME = 16
STRIP = 2 * FRAME
CORE = TW - 2 * LANE
SPAN = 96
DEPTH = SPAN + 2 * FRAME
MID = TH - 2 * FRAME
LEAD = 64
REST = MID - LEAD
REACH = LANE + 2 * FRAME
BF16 = jnp.bfloat16


def gauss_taps(sigma):
    spots = np.arange(-RG, RG + 1).astype(np.float64)
    raw = np.exp(-spots * spots / (2.0 * sigma * sigma))
    return [float(tap) for tap in np.float32(raw / raw.sum())[RG:]]


NARROW = gauss_taps(1.0)
BROAD = gauss_taps(2.0)


def split(values):
    high = values.astype(BF16)
    low = (values - high.astype(jnp.float32)).astype(BF16)
    return high, low


def bands(distance, frac):
    def look(spots):
        away = jnp.abs(spots)
        narrow = jnp.zeros(spots.shape, jnp.float32)
        broad = jnp.zeros(spots.shape, jnp.float32)
        for tap in range(RG + 1):
            here = away == tap
            narrow = jnp.where(here, NARROW[tap], narrow)
            broad = jnp.where(here, BROAD[tap], broad)
        return narrow, broad

    near = look(distance)
    far = look(distance - 1)
    return tuple((1.0 - frac) * a + frac * b for a, b in zip(near, far))


def column_weights(offset, pick):
    frac = (pick // 4).astype(jnp.float32) * 0.5 + 0.25
    shape = (REACH, LANE)
    window = lax.broadcasted_iota(jnp.int32, shape, 0)
    result = lax.broadcasted_iota(jnp.int32, shape, 1)
    narrow, broad = bands(window - result - (HW + offset), frac)
    weights = split(jnp.concatenate([narrow, narrow - broad], axis=1))
    zeros = jnp.zeros((2 * LANE - REACH, 2 * LANE), BF16)
    return tuple(jnp.concatenate([half, zeros], axis=0) for half in weights)


def row_weights(offset, pick):
    frac = (pick % 4).astype(jnp.float32) * 0.25 + 0.125
    shape = (SPAN, DEPTH)
    source = lax.broadcasted_iota(jnp.int32, shape, 1)
    result = lax.broadcasted_iota(jnp.int32, shape, 0)
    narrow, broad = bands(source - result - (FRAME + offset), frac)
    return split(jnp.concatenate([narrow - broad, broad], axis=1))


def product(left, right):
    dot = functools.partial(jnp.dot, preferred_element_type=jnp.float32)
    return dot(left[0], right[0]) + (dot(left[1], right[0]) + dot(left[0], right[1]))


def column_sums(windows, column):
    rows = windows[0].shape[0]
    sums = split(product(split(jnp.concatenate(windows, axis=0)), column))
    blocks = [slice(k * rows, (k + 1) * rows) for k in range(len(windows))]
    return [
        [jnp.concatenate([half[block, part] for block in blocks], axis=1) for half in sums]
        for part in (slice(0, LANE), slice(LANE, 2 * LANE))
    ]


def row_sums(row, sums, first=0):
    narrow, change = sums
    short = DEPTH - (narrow[0].shape[0] - first)
    filler = [jnp.zeros((short, narrow[0].shape[1]), BF16)] if short > 0 else []
    rows = slice(first, first + DEPTH)
    stacked = [jnp.concatenate([a[rows], *filler, b[rows], *filler], axis=0) for a, b in zip(narrow, change)]
    return product(row, stacked)


def core_windows(values):
    rolled = pltpu.roll(values, HW, 1)
    return [rolled[:, block * LANE : (block + 2) * LANE] for block in range(1, TW // LANE - 1)]


def lead_kernel(off_hbm, pick_hbm, x_hbm, lead, wh, wl, vh, vl, x, off, pick, sem):
    copies = [
        pltpu.make_async_copy(off_hbm, off, sem.at[0]),
        pltpu.make_async_copy(pick_hbm, pick, sem.at[1]),
        pltpu.make_async_copy(x_hbm.at[0, pl.ds(0, LEAD + 2 * FRAME)], x, sem.at[2]),
    ]
    for copy in copies:
        copy.start()
    copies[0].wait()
    copies[1].wait()
    column = column_weights(off[0, 0, 0, 1], pick[0, 0, 0])
    row = row_weights(off[0, 0, 0, 0], pick[0, 0, 0])
    wh[...], wl[...] = column
    vh[...], vl[...] = row
    copies[2].wait()
    sums = column_sums(core_windows(x[...]), column)
    lead[...] = row_sums([half[:LEAD] for half in row], sums)


def rest_kernel(x, wh, wl, vh, vl, rest, first, second):
    even = lax.axis_index("tx") % 2 == 0
    start, end = x[0, :, :LANE], x[0, :, TW - LANE :]
    first[...] = jnp.where(even, end, start)
    second[...] = jnp.where(even, start, end)
    column = (wh[...], wl[...])
    row = (vh[...], vl[...])
    sums = column_sums(core_windows(x[0, LEAD:, :]), column)
    rest[:SPAN, :] = row_sums(row, sums)
    last = REST - SPAN
    lower = [half[SPAN - last :] for half in row]
    rest[SPAN:, :] = row_sums(lower, sums, TH - DEPTH - LEAD)


def halos(axis, first, second):
    place = lax.axis_index(axis)
    inner = (place > 0) & (place < lax.axis_size(axis) - 1)
    even = place % 2 == 0
    second = jnp.where(inner, second, 0.0)
    return jnp.where(even, second, first), jnp.where(even, first, second)


def edge_block(before, after):
    lane = lax.broadcasted_iota(jnp.int32, before.shape, 1)
    return jnp.where(lane < LANE // 2, after, before)


def side_kernel(x, first, second, wh, wl, vh, vl, side, send_first, send_second):
    column = (wh[...], wl[...])
    row = (vh[...], vl[...])
    before, after = halos("tx", first[...], second[...])
    windows = [
        pltpu.roll(jnp.concatenate(strip, axis=1), 2 * LANE + HW, 1)[:, : 2 * LANE]
        for strip in ((before, x[0, :, : 2 * LANE]), (x[0, :, TW - 2 * LANE :], after))
    ]
    sums = column_sums(windows, column)
    side[:SPAN, :] = row_sums(row, sums)
    side[SPAN : 2 * SPAN, :] = row_sums(row, sums, SPAN)
    last = MID - 2 * SPAN
    lower = [half[SPAN - last :] for half in row]
    side[2 * SPAN :, :] = row_sums(lower, sums, TH - DEPTH)
    edge = edge_block(before, after)
    top = jnp.concatenate([x[0, :FRAME, :], edge[:FRAME]], axis=1)
    bottom = jnp.concatenate([x[0, TH - FRAME :, :], edge[TH - FRAME :]], axis=1)
    even = lax.axis_index("ty") % 2 == 0
    send_first[...] = jnp.where(even, bottom, top)
    send_second[...] = jnp.where(even, top, bottom)


def frame_kernel(x, first, second, row_first, row_second, wh, wl, vh, vl, frame):
    column = (wh[...], wl[...])
    top, bottom = halos("ty", row_first[...], row_second[...])
    own = []
    for rows in (slice(0, STRIP), slice(TH - STRIP, TH)):
        edge = edge_block(*halos("tx", first[rows, :], second[rows, :]))
        own.append(jnp.concatenate([x[0, rows, :], edge], axis=1))
    values = jnp.concatenate([top, own[0], own[1], bottom], axis=0)
    rolled = pltpu.roll(values, HW, 1)
    windows = [rolled[:, block * LANE : (block + 2) * LANE] for block in range(TW // LANE)]
    sums = column_sums(windows, column)
    below = values.shape[0] // 2
    row = [jnp.concatenate([half[:FRAME, :], half[below : below + FRAME, :]], axis=0) for half in (vh, vl)]
    frame[...] = row_sums(row, sums)


CHANGE_COST = 10**10
FAST = pl.BlockSpec(memory_space=pltpu.VMEM)
SLOW = pl.BlockSpec(memory_space=pltpu.HBM)
LIMIT = pltpu.CompilerParams(vmem_limit_bytes=16 * 2**20)


def f32(*shape):
    return jax.ShapeDtypeStruct(shape, jnp.float32)


def bf16(*shape):
    return jax.ShapeDtypeStruct(shape, BF16)


def cost(flops):
    return pl.CostEstimate(flops=flops, bytes_accessed=2**12, transcendentals=0)


def keep(array):
    return pltpu.with_memory_space_constraint(array, pltpu.HBM)


def lead_call(offsets, pick, raster):
    column = bf16(2 * LANE, 2 * LANE)
    row = bf16(SPAN, 2 * DEPTH)
    return pl.pallas_call(
        lead_kernel,
        out_shape=(f32(LEAD, CORE), column, column, row, row),
        in_specs=[SLOW] * 3,
        out_specs=(FAST,) * 5,
        scratch_shapes=[
            pltpu.VMEM((LEAD + 2 * FRAME, TW), jnp.float32),
            pltpu.SMEM(offsets.shape, jnp.int32),
            pltpu.SMEM(pick.shape, jnp.int32),
            pltpu.SemaphoreType.DMA((3,)),
        ],
        compiler_params=LIMIT,
        cost_estimate=cost(10**6),
        name="lead",
    )(keep(offsets), pick, keep(raster))


def fast_call(kernel, name, out_shape, *operands):
    many = isinstance(out_shape, tuple)
    return pl.pallas_call(
        kernel,
        out_shape=out_shape,
        in_specs=[FAST] * len(operands),
        out_specs=(FAST,) * len(out_shape) if many else FAST,
        compiler_params=LIMIT,
        cost_estimate=cost(10**6),
        name=name,
    )(*operands)


def change_kernel(places, count, fill, own_ref, *refs):
    others = refs[: 1 if count == 2 else 2]
    next_out, prev_out, value = refs[-4 - fill :][:3]
    sem = refs[-1]
    position = lax.axis_index("die")
    for out, there, forward in (
        (next_out, position < count - 1, True),
        (prev_out, position > 0, False),
    ):

        @pl.when(there)
        def _():
            own = own_ref[...]
            value[...] = others[0][...] - own if forward else own - others[-1][...]
            copies = [
                pltpu.make_async_copy(
                    value.at[pl.ds(row, tall), pl.ds(column, wide)],
                    out.at[0, pl.ds(out_row, tall), pl.ds(out_column, wide)],
                    sem.at[k],
                )
                for k, ((row, column), (out_row, out_column), (tall, wide)) in enumerate(places)
            ]
            for copy in copies:
                copy.start()
            for copy in copies:
                copy.wait()

        if fill:

            @pl.when(jnp.logical_not(there))
            def _():
                zeros = refs[-2]
                zeros[...] = jnp.zeros_like(zeros)
                copy = pltpu.make_async_copy(zeros, out.at[0], sem.at[0])
                copy.start()
                copy.wait()


def change_call(count, places, own, others, maps):
    operands = (own, *others)
    fill = not maps
    out = f32(1, TH, TW)
    return pl.pallas_call(
        functools.partial(change_kernel, places, count, fill),
        out_shape=(out, out),
        in_specs=[FAST] * len(operands) + [SLOW] * len(maps),
        out_specs=(SLOW, SLOW),
        scratch_shapes=[
            pltpu.VMEM(own.shape, jnp.float32),
            *([pltpu.VMEM((TH, TW), jnp.float32)] if fill else []),
            pltpu.SemaphoreType.DMA((len(places),)),
        ],
        input_output_aliases={len(operands) + k: k for k in range(len(maps))},
        compiler_params=LIMIT,
        cost_estimate=cost(CHANGE_COST),
        name="change",
    )(*operands, *maps)


LEAD_PLACES = (((0, 0), (FRAME, LANE), (LEAD, CORE)),)
REST_PLACES = (((0, 0), (FRAME + LEAD, LANE), (REST, CORE)),)
SIDE_PLACES = (((0, 0), (FRAME, 0), (MID, LANE)), ((0, LANE), (FRAME, TW - LANE), (MID, LANE)))
FRAME_PLACES = (((0, 0), (0, 0), (FRAME, TW)), ((FRAME, 0), (TH - FRAME, 0), (FRAME, TW)))


def swap_rounds(axis, first, second):
    count = lax.axis_size(axis)
    assert count % 2 == 0
    pairs = [(i, i ^ 1) for i in range(count)]
    others = [(i, min(max((i ^ 1) + 2 * (i % 2 * 2 - 1), 0), count - 1)) for i in range(count)]
    return lax.ppermute(first, axis, pairs), lax.ppermute(second, axis, others)


def other_dies(block):
    count = lax.axis_size("die")
    forward = [(i, i + 1) for i in range(count - 1)]
    backward = [(i + 1, i) for i in range(count - 1)]
    if count == 2:
        return (lax.ppermute(block, "die", forward + backward),)
    return (lax.ppermute(block, "die", backward), lax.ppermute(block, "die", forward))


def body(raster, shift_pick, offsets):
    count = lax.axis_size("die")
    lead, *weights = lead_call(offsets, shift_pick, raster)
    lead_others = other_dies(lead)
    strip = f32(TH, LANE)
    rest, first, second = fast_call(rest_kernel, "rest", (f32(REST, CORE), strip, strip), raster, *weights)
    rest_others = other_dies(rest)
    first, second = swap_rounds("tx", first, second)
    halo = f32(FRAME, TW + LANE)
    side, send_first, send_second = fast_call(
        side_kernel, "side", (f32(MID, 2 * LANE), halo, halo), raster, first, second, *weights
    )
    side_others = other_dies(side)
    row_first, row_second = swap_rounds("ty", send_first, send_second)
    frame = fast_call(
        frame_kernel, "frame", f32(STRIP, TW), raster, first, second, row_first, row_second, *weights
    )
    frame_others = other_dies(frame)
    maps = change_call(count, LEAD_PLACES, lead, lead_others, ())
    maps = change_call(count, REST_PLACES, rest, rest_others, maps)
    maps = change_call(count, SIDE_PLACES, side, side_others, maps)
    return tuple(change_call(count, FRAME_PLACES, frame, frame_others, maps))


def solution(mesh):
    in_specs = (P("die", "ty", "tx"), P("die", "ty", "tx"), P("die", "ty", "tx", None))
    out_specs = (P("die", "ty", "tx"), P("die", "ty", "tx"))
    return jax.shard_map(body, mesh=mesh, in_specs=in_specs, out_specs=out_specs, check_vma=False)
```

```python
import functools

import jax
import jax.numpy as jnp
import numpy as np
from jax import lax
from jax.experimental import pallas as pl
from jax.experimental.pallas import tpu as pltpu
from jax.sharding import PartitionSpec as P

TH = 256
TW = 1024
RG = 6
HW = 11
LANE = 128
FRAME = 16
STRIP = 2 * FRAME
CORE = TW - 2 * LANE
SPAN = 96
DEPTH = SPAN + 2 * FRAME
MID = TH - 2 * FRAME
LEAD = 64
REST = MID - LEAD
REACH = LANE + 2 * FRAME
BF16 = jnp.bfloat16


def gauss_taps(sigma):
    spots = np.arange(-RG, RG + 1).astype(np.float64)
    raw = np.exp(-spots * spots / (2.0 * sigma * sigma))
    return [float(tap) for tap in np.float32(raw / raw.sum())[RG:]]


NARROW = gauss_taps(1.0)
BROAD = gauss_taps(2.0)


def split(values):
    high = values.astype(BF16)
    low = (values - high.astype(jnp.float32)).astype(BF16)
    return high, low


def bands(distance, frac):
    def look(spots):
        away = jnp.abs(spots)
        narrow = jnp.zeros(spots.shape, jnp.float32)
        broad = jnp.zeros(spots.shape, jnp.float32)
        for tap in range(RG + 1):
            here = away == tap
            narrow = jnp.where(here, NARROW[tap], narrow)
            broad = jnp.where(here, BROAD[tap], broad)
        return narrow, broad

    near = look(distance)
    far = look(distance - 1)
    return tuple((1.0 - frac) * a + frac * b for a, b in zip(near, far))


def column_weights(offset, pick):
    frac = (pick // 4).astype(jnp.float32) * 0.5 + 0.25
    shape = (REACH, LANE)
    window = lax.broadcasted_iota(jnp.int32, shape, 0)
    result = lax.broadcasted_iota(jnp.int32, shape, 1)
    narrow, broad = bands(window - result - (HW + offset), frac)
    weights = split(jnp.concatenate([narrow, narrow - broad], axis=1))
    zeros = jnp.zeros((2 * LANE - REACH, 2 * LANE), BF16)
    return tuple(jnp.concatenate([half, zeros], axis=0) for half in weights)


def row_weights(offset, pick):
    frac = (pick % 4).astype(jnp.float32) * 0.25 + 0.125
    shape = (SPAN, DEPTH)
    source = lax.broadcasted_iota(jnp.int32, shape, 1)
    result = lax.broadcasted_iota(jnp.int32, shape, 0)
    narrow, broad = bands(source - result - (FRAME + offset), frac)
    return split(jnp.concatenate([narrow - broad, broad], axis=1))


def product(left, right):
    dot = functools.partial(jnp.dot, preferred_element_type=jnp.float32)
    return dot(left[0], right[0]) + (dot(left[1], right[0]) + dot(left[0], right[1]))


def column_sums(windows, column):
    rows = windows[0].shape[0]
    sums = split(product(split(jnp.concatenate(windows, axis=0)), column))
    blocks = [slice(k * rows, (k + 1) * rows) for k in range(len(windows))]
    return [
        [jnp.concatenate([half[block, part] for block in blocks], axis=1) for half in sums]
        for part in (slice(0, LANE), slice(LANE, 2 * LANE))
    ]


def row_sums(row, sums, first=0):
    narrow, change = sums
    short = DEPTH - (narrow[0].shape[0] - first)
    filler = [jnp.zeros((short, narrow[0].shape[1]), BF16)] if short > 0 else []
    rows = slice(first, first + DEPTH)
    stacked = [jnp.concatenate([a[rows], *filler, b[rows], *filler], axis=0) for a, b in zip(narrow, change)]
    return product(row, stacked)


def core_windows(values):
    rolled = pltpu.roll(values, HW, 1)
    return [rolled[:, block * LANE : (block + 2) * LANE] for block in range(1, TW // LANE - 1)]


def lead_kernel(off_ref, pick_ref, x_hbm, lead, x, wh, wl, vh, vl, sem):
    need = LEAD + 2 * FRAME
    parts = [pl.ds(0, need), pl.ds(need, TH - need)]
    copies = [
        pltpu.make_async_copy(x_hbm.at[0, rows], x.at[rows], sem.at[k]) for k, rows in enumerate(parts)
    ]
    for copy in copies:
        copy.start()
    offsets = off_ref[0, 0]
    pick = pick_ref[0, 0, 0]
    column = column_weights(offsets[:, 1:], pick)
    row = row_weights(offsets[:, :1], pick)
    wh[...], wl[...] = column
    vh[...], vl[...] = row
    copies[0].wait()
    sums = column_sums(core_windows(x[:need, :]), column)
    lead[...] = row_sums([half[:LEAD] for half in row], sums)
    copies[1].wait()


def rest_kernel(x, wh, wl, vh, vl, rest, first, second):
    even = lax.axis_index("tx") % 2 == 0
    start = x[:, :LANE].T[:FRAME]
    end = x[:, TW - LANE :].T[LANE - FRAME :]
    first[...] = jnp.where(even, end, start)
    second[...] = jnp.where(even, start, end)
    column = (wh[...], wl[...])
    row = (vh[...], vl[...])
    sums = column_sums(core_windows(x[LEAD:, :]), column)
    rest[:SPAN, :] = row_sums(row, sums)
    last = REST - SPAN
    lower = [half[SPAN - last :] for half in row]
    rest[SPAN:, :] = row_sums(lower, sums, TH - DEPTH - LEAD)


def halos(axis, first, second):
    place = lax.axis_index(axis)
    inner = (place > 0) & (place < lax.axis_size(axis) - 1)
    even = place % 2 == 0
    second = jnp.where(inner, second, 0.0)
    return jnp.where(even, second, first), jnp.where(even, first, second)


def side_kernel(x, first, second, wh, wl, vh, vl, side, send_first, send_second, edge_ref):
    column = (wh[...], wl[...])
    row = (vh[...], vl[...])
    before, after = halos("tx", first[...], second[...])
    filler = jnp.zeros((LANE - 2 * FRAME, TH), jnp.float32)
    edge = jnp.concatenate([after, filler, before], axis=0).T
    edge_ref[...] = edge
    windows = [
        pltpu.roll(jnp.concatenate(strip, axis=1), 2 * LANE + HW, 1)[:, : 2 * LANE]
        for strip in ((edge, x[:, : 2 * LANE]), (x[:, TW - 2 * LANE :], edge))
    ]
    sums = column_sums(windows, column)
    side[:SPAN, :] = row_sums(row, sums)
    side[SPAN : 2 * SPAN, :] = row_sums(row, sums, SPAN)
    last = MID - 2 * SPAN
    lower = [half[SPAN - last :] for half in row]
    side[2 * SPAN :, :] = row_sums(lower, sums, TH - DEPTH)
    top = jnp.concatenate([x[:FRAME, :], edge[:FRAME]], axis=1)
    bottom = jnp.concatenate([x[TH - FRAME :, :], edge[TH - FRAME :]], axis=1)
    even = lax.axis_index("ty") % 2 == 0
    send_first[...] = jnp.where(even, bottom, top)
    send_second[...] = jnp.where(even, top, bottom)


def frame_kernel(x, edge, row_first, row_second, wh, wl, vh, vl, frame):
    column = (wh[...], wl[...])
    top, bottom = halos("ty", row_first[...], row_second[...])
    own = [
        jnp.concatenate([x[rows, :], edge[rows, :]], axis=1)
        for rows in (slice(0, STRIP), slice(TH - STRIP, TH))
    ]
    values = jnp.concatenate([top, own[0], own[1], bottom], axis=0)
    rolled = pltpu.roll(values, HW, 1)
    windows = [rolled[:, block * LANE : (block + 2) * LANE] for block in range(TW // LANE)]
    sums = column_sums(windows, column)
    below = values.shape[0] // 2
    row = [jnp.concatenate([half[:FRAME, :], half[below : below + FRAME, :]], axis=0) for half in (vh, vl)]
    frame[...] = row_sums(row, sums)


COSTS = (4 * 10**9, 10**10, 10**10, 10**10)
FAST = pl.BlockSpec(memory_space=pltpu.VMEM)
SLOW = pl.BlockSpec(memory_space=pltpu.HBM)
LIMIT = pltpu.CompilerParams(vmem_limit_bytes=16 * 2**20)


def f32(*shape):
    return jax.ShapeDtypeStruct(shape, jnp.float32)


def bf16(*shape):
    return jax.ShapeDtypeStruct(shape, BF16)


def cost(flops):
    return pl.CostEstimate(flops=flops, bytes_accessed=2**12, transcendentals=0)


def keep(array):
    return pltpu.with_memory_space_constraint(array, pltpu.HBM)


def lead_call(offsets, pick, raster):
    column = bf16(2 * LANE, 2 * LANE)
    row = bf16(SPAN, 2 * DEPTH)
    return pl.pallas_call(
        lead_kernel,
        out_shape=(f32(LEAD, CORE), f32(TH, TW), column, column, row, row),
        in_specs=[FAST, pl.BlockSpec(memory_space=pltpu.SMEM), SLOW],
        out_specs=(FAST,) * 6,
        scratch_shapes=[pltpu.SemaphoreType.DMA((2,))],
        compiler_params=LIMIT,
        cost_estimate=cost(10**6),
        name="lead",
    )(offsets, pick, keep(raster))


def fast_call(kernel, name, out_shape, *operands):
    many = isinstance(out_shape, tuple)
    return pl.pallas_call(
        kernel,
        out_shape=out_shape,
        in_specs=[FAST] * len(operands),
        out_specs=(FAST,) * len(out_shape) if many else FAST,
        compiler_params=LIMIT,
        cost_estimate=cost(10**6),
        name=name,
    )(*operands)


def change_kernel(places, count, fill, own_ref, *refs):
    others = refs[: 1 if count == 2 else 2]
    next_out, prev_out, value = refs[-4 - fill :][:3]
    sem = refs[-1]
    position = lax.axis_index("die")
    for out, there, forward in (
        (next_out, position < count - 1, True),
        (prev_out, position > 0, False),
    ):

        @pl.when(there)
        def _():
            own = own_ref[...]
            value[...] = others[0][...] - own if forward else own - others[-1][...]
            copies = [
                pltpu.make_async_copy(
                    value.at[pl.ds(row, tall), pl.ds(column, wide)],
                    out.at[0, pl.ds(out_row, tall), pl.ds(out_column, wide)],
                    sem.at[k],
                )
                for k, ((row, column), (out_row, out_column), (tall, wide)) in enumerate(places)
            ]
            for copy in copies:
                copy.start()
            for copy in copies:
                copy.wait()

        if fill:

            @pl.when(jnp.logical_not(there))
            def _():
                zeros = refs[-2]
                zeros[...] = jnp.zeros_like(zeros)
                copy = pltpu.make_async_copy(zeros, out.at[0], sem.at[0])
                copy.start()
                copy.wait()


def change_call(count, places, flops, own, others, maps):
    operands = (own, *others)
    fill = not maps
    out = f32(1, TH, TW)
    return pl.pallas_call(
        functools.partial(change_kernel, places, count, fill),
        out_shape=(out, out),
        in_specs=[FAST] * len(operands) + [SLOW] * len(maps),
        out_specs=(SLOW, SLOW),
        scratch_shapes=[
            pltpu.VMEM(own.shape, jnp.float32),
            *([pltpu.VMEM((TH, TW), jnp.float32)] if fill else []),
            pltpu.SemaphoreType.DMA((len(places),)),
        ],
        input_output_aliases={len(operands) + k: k for k in range(len(maps))},
        compiler_params=LIMIT,
        cost_estimate=cost(flops),
        name="change",
    )(*operands, *maps)


LEAD_PLACES = (((0, 0), (FRAME, LANE), (LEAD, CORE)),)
REST_PLACES = (((0, 0), (FRAME + LEAD, LANE), (REST, CORE)),)
SIDE_PLACES = (((0, 0), (FRAME, 0), (MID, LANE)), ((0, LANE), (FRAME, TW - LANE), (MID, LANE)))
FRAME_PLACES = (((0, 0), (0, 0), (FRAME, TW)), ((FRAME, 0), (TH - FRAME, 0), (FRAME, TW)))


def swap_rounds(axis, first, second):
    count = lax.axis_size(axis)
    assert count % 2 == 0
    pairs = [(i, i ^ 1) for i in range(count)]
    others = [(i, min(max((i ^ 1) + 2 * (i % 2 * 2 - 1), 0), count - 1)) for i in range(count)]
    return lax.ppermute(first, axis, pairs), lax.ppermute(second, axis, others)


def other_dies(block):
    count = lax.axis_size("die")
    forward = [(i, i + 1) for i in range(count - 1)]
    backward = [(i + 1, i) for i in range(count - 1)]
    if count == 2:
        return (lax.ppermute(block, "die", forward + backward),)
    return (lax.ppermute(block, "die", backward), lax.ppermute(block, "die", forward))


def body(raster, shift_pick, offsets):
    count = lax.axis_size("die")
    lead, tile, *weights = lead_call(offsets, shift_pick, raster)
    lead_others = other_dies(lead)
    strip = f32(FRAME, TH)
    rest, first, second = fast_call(rest_kernel, "rest", (f32(REST, CORE), strip, strip), tile, *weights)
    rest_others = other_dies(rest)
    first, second = swap_rounds("tx", first, second)
    halo = f32(FRAME, TW + LANE)
    side, send_first, send_second, edge = fast_call(
        side_kernel, "side", (f32(MID, 2 * LANE), halo, halo, f32(TH, LANE)), tile, first, second, *weights
    )
    side_others = other_dies(side)
    row_first, row_second = swap_rounds("ty", send_first, send_second)
    frame = fast_call(
        frame_kernel, "frame", f32(STRIP, TW), tile, edge, row_first, row_second, *weights
    )
    frame_others = other_dies(frame)
    maps = change_call(count, LEAD_PLACES, COSTS[0], lead, lead_others, ())
    maps = change_call(count, REST_PLACES, COSTS[1], rest, rest_others, maps)
    maps = change_call(count, SIDE_PLACES, COSTS[2], side, side_others, maps)
    return tuple(change_call(count, FRAME_PLACES, COSTS[3], frame, frame_others, maps))


def solution(mesh):
    in_specs = (P("die", "ty", "tx"), P("die", "ty", "tx"), P("die", "ty", "tx", None))
    out_specs = (P("die", "ty", "tx"), P("die", "ty", "tx"))
    return jax.shard_map(body, mesh=mesh, in_specs=in_specs, out_specs=out_specs, check_vma=False)
```

```python
import functools

import jax
import jax.numpy as jnp
import numpy as np
from jax import lax
from jax.experimental import pallas as pl
from jax.experimental.pallas import tpu as pltpu
from jax.sharding import PartitionSpec as P

TH = 256
TW = 1024
RG = 6
HW = 11
LANE = 128
FRAME = 16
STRIP = 2 * FRAME
CORE = TW - 2 * LANE
SPAN = 96
DEPTH = SPAN + 2 * FRAME
MID = TH - 2 * FRAME
LEAD = 64
REST = MID - LEAD
REACH = LANE + 2 * FRAME
BF16 = jnp.bfloat16


def gauss_taps(sigma):
    spots = np.arange(-RG, RG + 1).astype(np.float64)
    raw = np.exp(-spots * spots / (2.0 * sigma * sigma))
    return [float(tap) for tap in np.float32(raw / raw.sum())[RG:]]


NARROW = gauss_taps(1.0)
BROAD = gauss_taps(2.0)


def split(values):
    high = values.astype(BF16)
    low = (values - high.astype(jnp.float32)).astype(BF16)
    return high, low


def bands(distance, frac):
    def look(spots):
        away = jnp.abs(spots)
        narrow = jnp.zeros(spots.shape, jnp.float32)
        broad = jnp.zeros(spots.shape, jnp.float32)
        for tap in range(RG + 1):
            here = away == tap
            narrow = jnp.where(here, NARROW[tap], narrow)
            broad = jnp.where(here, BROAD[tap], broad)
        return narrow, broad

    near = look(distance)
    far = look(distance - 1)
    return tuple((1.0 - frac) * a + frac * b for a, b in zip(near, far))


def column_weights(offset, pick):
    frac = (pick // 4).astype(jnp.float32) * 0.5 + 0.25
    shape = (REACH, LANE)
    window = lax.broadcasted_iota(jnp.int32, shape, 0)
    result = lax.broadcasted_iota(jnp.int32, shape, 1)
    narrow, broad = bands(window - result - (HW + offset), frac)
    weights = split(jnp.concatenate([narrow, narrow - broad], axis=1))
    zeros = jnp.zeros((2 * LANE - REACH, 2 * LANE), BF16)
    return tuple(jnp.concatenate([half, zeros], axis=0) for half in weights)


def row_weights(offset, pick):
    frac = (pick % 4).astype(jnp.float32) * 0.25 + 0.125
    shape = (SPAN, DEPTH)
    source = lax.broadcasted_iota(jnp.int32, shape, 1)
    result = lax.broadcasted_iota(jnp.int32, shape, 0)
    narrow, broad = bands(source - result - (FRAME + offset), frac)
    return split(jnp.concatenate([narrow - broad, broad], axis=1))


def product(left, right):
    dot = functools.partial(jnp.dot, preferred_element_type=jnp.float32)
    return dot(left[0], right[0]) + (dot(left[1], right[0]) + dot(left[0], right[1]))


def column_sums(windows, column):
    rows = windows[0].shape[0]
    sums = split(product(split(jnp.concatenate(windows, axis=0)), column))
    blocks = [slice(k * rows, (k + 1) * rows) for k in range(len(windows))]
    return [
        [jnp.concatenate([half[block, part] for block in blocks], axis=1) for half in sums]
        for part in (slice(0, LANE), slice(LANE, 2 * LANE))
    ]


def row_sums(row, sums, first=0):
    narrow, change = sums
    short = DEPTH - (narrow[0].shape[0] - first)
    filler = [jnp.zeros((short, narrow[0].shape[1]), BF16)] if short > 0 else []
    rows = slice(first, first + DEPTH)
    stacked = [jnp.concatenate([a[rows], *filler, b[rows], *filler], axis=0) for a, b in zip(narrow, change)]
    return product(row, stacked)


def core_windows(values):
    rolled = pltpu.roll(values, HW, 1)
    return [rolled[:, block * LANE : (block + 2) * LANE] for block in range(1, TW // LANE - 1)]


def weights_kernel(off_ref, pick_ref, wh, wl, vh, vl):
    offsets = off_ref[0, 0]
    pick = pick_ref[0, 0, 0]
    wh[...], wl[...] = column_weights(offsets[:, 1:], pick)
    vh[...], vl[...] = row_weights(offsets[:, :1], pick)


def lead_kernel(x, wh, wl, vh, vl, lead):
    sums = column_sums(core_windows(x[0, : LEAD + 2 * FRAME, :]), (wh[...], wl[...]))
    lead[...] = row_sums([half[:LEAD, :] for half in (vh, vl)], sums)


def rest_kernel(x, wh, wl, vh, vl, rest, first, second):
    even = lax.axis_index("tx") % 2 == 0
    start = x[0, :, :LANE].T[:FRAME]
    end = x[0, :, TW - LANE :].T[LANE - FRAME :]
    first[...] = jnp.where(even, end, start)
    second[...] = jnp.where(even, start, end)
    column = (wh[...], wl[...])
    row = (vh[...], vl[...])
    sums = column_sums(core_windows(x[0, LEAD:, :]), column)
    rest[:SPAN, :] = row_sums(row, sums)
    last = REST - SPAN
    lower = [half[SPAN - last :] for half in row]
    rest[SPAN:, :] = row_sums(lower, sums, TH - DEPTH - LEAD)


def halos(axis, first, second):
    place = lax.axis_index(axis)
    inner = (place > 0) & (place < lax.axis_size(axis) - 1)
    even = place % 2 == 0
    second = jnp.where(inner, second, 0.0)
    return jnp.where(even, second, first), jnp.where(even, first, second)


def side_kernel(x, first, second, wh, wl, vh, vl, side, send_first, send_second, edge_ref):
    column = (wh[...], wl[...])
    row = (vh[...], vl[...])
    before, after = halos("tx", first[...], second[...])
    filler = jnp.zeros((LANE - 2 * FRAME, TH), jnp.float32)
    edge = jnp.concatenate([after, filler, before], axis=0).T
    edge_ref[...] = edge
    windows = [
        pltpu.roll(jnp.concatenate(strip, axis=1), 2 * LANE + HW, 1)[:, : 2 * LANE]
        for strip in ((edge, x[0, :, : 2 * LANE]), (x[0, :, TW - 2 * LANE :], edge))
    ]
    sums = column_sums(windows, column)
    side[:SPAN, :] = row_sums(row, sums)
    side[SPAN : 2 * SPAN, :] = row_sums(row, sums, SPAN)
    last = MID - 2 * SPAN
    lower = [half[SPAN - last :] for half in row]
    side[2 * SPAN :, :] = row_sums(lower, sums, TH - DEPTH)
    top = jnp.concatenate([x[0, :FRAME, :], edge[:FRAME]], axis=1)
    bottom = jnp.concatenate([x[0, TH - FRAME :, :], edge[TH - FRAME :]], axis=1)
    even = lax.axis_index("ty") % 2 == 0
    send_first[...] = jnp.where(even, bottom, top)
    send_second[...] = jnp.where(even, top, bottom)


def frame_kernel(x, edge, row_first, row_second, wh, wl, vh, vl, frame):
    column = (wh[...], wl[...])
    top, bottom = halos("ty", row_first[...], row_second[...])
    own = [
        jnp.concatenate([x[0, rows, :], edge[rows, :]], axis=1)
        for rows in (slice(0, STRIP), slice(TH - STRIP, TH))
    ]
    values = jnp.concatenate([top, own[0], own[1], bottom], axis=0)
    rolled = pltpu.roll(values, HW, 1)
    windows = [rolled[:, block * LANE : (block + 2) * LANE] for block in range(TW // LANE)]
    sums = column_sums(windows, column)
    below = values.shape[0] // 2
    row = [jnp.concatenate([half[:FRAME, :], half[below : below + FRAME, :]], axis=0) for half in (vh, vl)]
    frame[...] = row_sums(row, sums)


COSTS = (4 * 10**9, 10**10, 10**10, 10**10)
FAST = pl.BlockSpec(memory_space=pltpu.VMEM)
SLOW = pl.BlockSpec(memory_space=pltpu.HBM)
LIMIT = pltpu.CompilerParams(vmem_limit_bytes=16 * 2**20)


def f32(*shape):
    return jax.ShapeDtypeStruct(shape, jnp.float32)


def bf16(*shape):
    return jax.ShapeDtypeStruct(shape, BF16)


def cost(flops):
    return pl.CostEstimate(flops=flops, bytes_accessed=2**12, transcendentals=0)


def weights_call(offsets, pick):
    column = bf16(2 * LANE, 2 * LANE)
    row = bf16(SPAN, 2 * DEPTH)
    return pl.pallas_call(
        weights_kernel,
        out_shape=(column, column, row, row),
        in_specs=[FAST, pl.BlockSpec(memory_space=pltpu.SMEM)],
        out_specs=(FAST,) * 4,
        compiler_params=LIMIT,
        cost_estimate=cost(4 * 10**8),
        name="weights",
    )(offsets, pick)


def fast_call(kernel, name, out_shape, *operands):
    many = isinstance(out_shape, tuple)
    return pl.pallas_call(
        kernel,
        out_shape=out_shape,
        in_specs=[FAST] * len(operands),
        out_specs=(FAST,) * len(out_shape) if many else FAST,
        compiler_params=LIMIT,
        cost_estimate=cost(10**6),
        name=name,
    )(*operands)


def change_kernel(places, count, fill, own_ref, *refs):
    others = refs[: 1 if count == 2 else 2]
    next_out, prev_out, value = refs[-4 - fill :][:3]
    sem = refs[-1]
    position = lax.axis_index("die")
    for out, there, forward in (
        (next_out, position < count - 1, True),
        (prev_out, position > 0, False),
    ):

        @pl.when(there)
        def _():
            own = own_ref[...]
            value[...] = others[0][...] - own if forward else own - others[-1][...]
            copies = [
                pltpu.make_async_copy(
                    value.at[pl.ds(row, tall), pl.ds(column, wide)],
                    out.at[0, pl.ds(out_row, tall), pl.ds(out_column, wide)],
                    sem.at[k],
                )
                for k, ((row, column), (out_row, out_column), (tall, wide)) in enumerate(places)
            ]
            for copy in copies:
                copy.start()
            for copy in copies:
                copy.wait()

        if fill:

            @pl.when(jnp.logical_not(there))
            def _():
                zeros = refs[-2]
                zeros[...] = jnp.zeros_like(zeros)
                copy = pltpu.make_async_copy(zeros, out.at[0], sem.at[0])
                copy.start()
                copy.wait()


def change_call(count, places, flops, own, others, maps):
    operands = (own, *others)
    fill = not maps
    out = f32(1, TH, TW)
    return pl.pallas_call(
        functools.partial(change_kernel, places, count, fill),
        out_shape=(out, out),
        in_specs=[FAST] * len(operands) + [SLOW] * len(maps),
        out_specs=(SLOW, SLOW),
        scratch_shapes=[
            pltpu.VMEM(own.shape, jnp.float32),
            *([pltpu.VMEM((TH, TW), jnp.float32)] if fill else []),
            pltpu.SemaphoreType.DMA((len(places),)),
        ],
        input_output_aliases={len(operands) + k: k for k in range(len(maps))},
        compiler_params=LIMIT,
        cost_estimate=cost(flops),
        name="change",
    )(*operands, *maps)


LEAD_PLACES = (((0, 0), (FRAME, LANE), (LEAD, CORE)),)
REST_PLACES = (((0, 0), (FRAME + LEAD, LANE), (REST, CORE)),)
SIDE_PLACES = (((0, 0), (FRAME, 0), (MID, LANE)), ((0, LANE), (FRAME, TW - LANE), (MID, LANE)))
FRAME_PLACES = (((0, 0), (0, 0), (FRAME, TW)), ((FRAME, 0), (TH - FRAME, 0), (FRAME, TW)))


def swap_rounds(axis, first, second):
    count = lax.axis_size(axis)
    assert count % 2 == 0
    pairs = [(i, i ^ 1) for i in range(count)]
    others = [(i, min(max((i ^ 1) + 2 * (i % 2 * 2 - 1), 0), count - 1)) for i in range(count)]
    return lax.ppermute(first, axis, pairs), lax.ppermute(second, axis, others)


def other_dies(block):
    count = lax.axis_size("die")
    forward = [(i, i + 1) for i in range(count - 1)]
    backward = [(i + 1, i) for i in range(count - 1)]
    if count == 2:
        return (lax.ppermute(block, "die", forward + backward),)
    return (lax.ppermute(block, "die", backward), lax.ppermute(block, "die", forward))


def body(raster, shift_pick, offsets):
    count = lax.axis_size("die")
    weights = weights_call(offsets, shift_pick)
    lead = fast_call(lead_kernel, "lead", f32(LEAD, CORE), raster, *weights)
    lead_others = other_dies(lead)
    strip = f32(FRAME, TH)
    rest, first, second = fast_call(rest_kernel, "rest", (f32(REST, CORE), strip, strip), raster, *weights)
    rest_others = other_dies(rest)
    first, second = swap_rounds("tx", first, second)
    halo = f32(FRAME, TW + LANE)
    side, send_first, send_second, edge = fast_call(
        side_kernel, "side", (f32(MID, 2 * LANE), halo, halo, f32(TH, LANE)), raster, first, second, *weights
    )
    side_others = other_dies(side)
    row_first, row_second = swap_rounds("ty", send_first, send_second)
    frame = fast_call(
        frame_kernel, "frame", f32(STRIP, TW), raster, edge, row_first, row_second, *weights
    )
    frame_others = other_dies(frame)
    maps = change_call(count, LEAD_PLACES, COSTS[0], lead, lead_others, ())
    maps = change_call(count, REST_PLACES, COSTS[1], rest, rest_others, maps)
    maps = change_call(count, SIDE_PLACES, COSTS[2], side, side_others, maps)
    return tuple(change_call(count, FRAME_PLACES, COSTS[3], frame, frame_others, maps))


def solution(mesh):
    in_specs = (P("die", "ty", "tx"), P("die", "ty", "tx"), P("die", "ty", "tx", None))
    out_specs = (P("die", "ty", "tx"), P("die", "ty", "tx"))
    return jax.shard_map(body, mesh=mesh, in_specs=in_specs, out_specs=out_specs, check_vma=False)
```

```python
import functools

import jax
import jax.numpy as jnp
import numpy as np
from jax import lax
from jax.experimental import pallas as pl
from jax.experimental.pallas import tpu as pltpu
from jax.sharding import PartitionSpec as P

TH = 256
TW = 1024
RG = 6
HW = 11
LANE = 128
FRAME = 16
STRIP = 2 * FRAME
CORE = TW - 2 * LANE
SPAN = 96
DEPTH = SPAN + 2 * FRAME
MID = TH - 2 * FRAME
LEAD = 48
REST = MID - LEAD
REACH = LANE + 2 * FRAME
BF16 = jnp.bfloat16


def gauss_taps(sigma):
    spots = np.arange(-RG, RG + 1).astype(np.float64)
    raw = np.exp(-spots * spots / (2.0 * sigma * sigma))
    return [float(tap) for tap in np.float32(raw / raw.sum())[RG:]]


NARROW = gauss_taps(1.0)
BROAD = gauss_taps(2.0)


def split(values):
    high = values.astype(BF16)
    low = (values - high.astype(jnp.float32)).astype(BF16)
    return high, low


def bands(distance, frac):
    def look(spots):
        away = jnp.abs(spots)
        narrow = jnp.zeros(spots.shape, jnp.float32)
        broad = jnp.zeros(spots.shape, jnp.float32)
        for tap in range(RG + 1):
            here = away == tap
            narrow = jnp.where(here, NARROW[tap], narrow)
            broad = jnp.where(here, BROAD[tap], broad)
        return narrow, broad

    near = look(distance)
    far = look(distance - 1)
    return tuple((1.0 - frac) * a + frac * b for a, b in zip(near, far))


def column_weights(offset, pick):
    frac = (pick // 4).astype(jnp.float32) * 0.5 + 0.25
    shape = (REACH, LANE)
    window = lax.broadcasted_iota(jnp.int32, shape, 0)
    result = lax.broadcasted_iota(jnp.int32, shape, 1)
    narrow, broad = bands(window - result - (HW + offset), frac)
    weights = split(jnp.concatenate([narrow, narrow - broad], axis=1))
    zeros = jnp.zeros((2 * LANE - REACH, 2 * LANE), BF16)
    return tuple(jnp.concatenate([half, zeros], axis=0) for half in weights)


def row_weights(offset, pick):
    frac = (pick % 4).astype(jnp.float32) * 0.25 + 0.125
    shape = (SPAN, DEPTH)
    source = lax.broadcasted_iota(jnp.int32, shape, 1)
    result = lax.broadcasted_iota(jnp.int32, shape, 0)
    narrow, broad = bands(source - result - (FRAME + offset), frac)
    return split(jnp.concatenate([narrow - broad, broad], axis=1))


def product(left, right):
    dot = functools.partial(jnp.dot, preferred_element_type=jnp.float32)
    return dot(left[0], right[0]) + (dot(left[1], right[0]) + dot(left[0], right[1]))


def column_sums(windows, column):
    rows = windows[0].shape[0]
    sums = split(product(split(jnp.concatenate(windows, axis=0)), column))
    blocks = [slice(k * rows, (k + 1) * rows) for k in range(len(windows))]
    return [
        [jnp.concatenate([half[block, part] for block in blocks], axis=1) for half in sums]
        for part in (slice(0, LANE), slice(LANE, 2 * LANE))
    ]


def row_sums(row, sums, first=0):
    narrow, change = sums
    short = DEPTH - (narrow[0].shape[0] - first)
    filler = [jnp.zeros((short, narrow[0].shape[1]), BF16)] if short > 0 else []
    rows = slice(first, first + DEPTH)
    stacked = [jnp.concatenate([a[rows], *filler, b[rows], *filler], axis=0) for a, b in zip(narrow, change)]
    return product(row, stacked)


def core_windows(values, level):
    rolled = pltpu.roll(values - level, HW, 1)
    return [rolled[:, block * LANE : (block + 2) * LANE] for block in range(1, TW // LANE - 1)]


def weights_kernel(off_ref, pick_ref, wh, wl, vh, vl):
    offsets = off_ref[0, 0]
    pick = pick_ref[0, 0, 0]
    wh[...], wl[...] = column_weights(offsets[:, 1:], pick)
    vh[...], vl[...] = row_weights(offsets[:, :1], pick)


def lead_kernel(x, wh, wl, vh, vl, lead, level_ref):
    total = jnp.sum(jnp.sum(x[0, :8, :], axis=0, keepdims=True), axis=1, keepdims=True)
    level = total * (1.0 / (8 * TW))
    level_ref[...] = jnp.broadcast_to(level, level_ref.shape)
    sums = column_sums(core_windows(x[0, : LEAD + 2 * FRAME, :], level), (wh[...], wl[...]))
    lead[...] = row_sums([half[:LEAD, :] for half in (vh, vl)], sums)


def rest_kernel(x, level_ref, wh, wl, vh, vl, rest, first, second):
    even = lax.axis_index("tx") % 2 == 0
    start = x[0, :, :LANE].T[:FRAME]
    end = x[0, :, TW - LANE :].T[LANE - FRAME :]
    first[...] = jnp.where(even, end, start)
    second[...] = jnp.where(even, start, end)
    column = (wh[...], wl[...])
    row = (vh[...], vl[...])
    sums = column_sums(core_windows(x[0, LEAD:, :], level_ref[:1, :1]), column)
    rest[:SPAN, :] = row_sums(row, sums)
    last = REST - SPAN
    lower = [half[SPAN - last :] for half in row]
    rest[SPAN:, :] = row_sums(lower, sums, TH - DEPTH - LEAD)


def halos(axis, first, second):
    place = lax.axis_index(axis)
    inner = (place > 0) & (place < lax.axis_size(axis) - 1)
    even = place % 2 == 0
    second = jnp.where(inner, second, 0.0)
    return jnp.where(even, second, first), jnp.where(even, first, second)


def side_kernel(x, level_ref, first, second, wh, wl, vh, vl, side, send_first, send_second, edge_ref):
    column = (wh[...], wl[...])
    row = (vh[...], vl[...])
    before, after = halos("tx", first[...], second[...])
    filler = jnp.zeros((LANE - 2 * FRAME, TH), jnp.float32)
    edge = jnp.concatenate([after, filler, before], axis=0).T
    edge_ref[...] = edge
    windows = [
        pltpu.roll(jnp.concatenate(strip, axis=1) - level_ref[:1, :1], 2 * LANE + HW, 1)[:, : 2 * LANE]
        for strip in ((edge, x[0, :, : 2 * LANE]), (x[0, :, TW - 2 * LANE :], edge))
    ]
    sums = column_sums(windows, column)
    side[:SPAN, :] = row_sums(row, sums)
    side[SPAN : 2 * SPAN, :] = row_sums(row, sums, SPAN)
    last = MID - 2 * SPAN
    lower = [half[SPAN - last :] for half in row]
    side[2 * SPAN :, :] = row_sums(lower, sums, TH - DEPTH)
    top = jnp.concatenate([x[0, :FRAME, :], edge[:FRAME]], axis=1)
    bottom = jnp.concatenate([x[0, TH - FRAME :, :], edge[TH - FRAME :]], axis=1)
    even = lax.axis_index("ty") % 2 == 0
    send_first[...] = jnp.where(even, bottom, top)
    send_second[...] = jnp.where(even, top, bottom)


def frame_kernel(x, level_ref, edge, row_first, row_second, wh, wl, vh, vl, frame):
    column = (wh[...], wl[...])
    top, bottom = halos("ty", row_first[...], row_second[...])
    own = [
        jnp.concatenate([x[0, rows, :], edge[rows, :]], axis=1)
        for rows in (slice(0, STRIP), slice(TH - STRIP, TH))
    ]
    values = jnp.concatenate([top, own[0], own[1], bottom], axis=0)
    rolled = pltpu.roll(values - level_ref[:1, :1], HW, 1)
    windows = [rolled[:, block * LANE : (block + 2) * LANE] for block in range(TW // LANE)]
    sums = column_sums(windows, column)
    below = values.shape[0] // 2
    row = [jnp.concatenate([half[:FRAME, :], half[below : below + FRAME, :]], axis=0) for half in (vh, vl)]
    frame[...] = row_sums(row, sums)


COSTS = (44 * 10**8, 10**10, 10**10, 10**10)
FAST = pl.BlockSpec(memory_space=pltpu.VMEM)
SLOW = pl.BlockSpec(memory_space=pltpu.HBM)
LIMIT = pltpu.CompilerParams(vmem_limit_bytes=16 * 2**20)


def f32(*shape):
    return jax.ShapeDtypeStruct(shape, jnp.float32)


def bf16(*shape):
    return jax.ShapeDtypeStruct(shape, BF16)


def cost(flops):
    return pl.CostEstimate(flops=flops, bytes_accessed=2**12, transcendentals=0)


def weights_call(offsets, pick):
    column = bf16(2 * LANE, 2 * LANE)
    row = bf16(SPAN, 2 * DEPTH)
    return pl.pallas_call(
        weights_kernel,
        out_shape=(column, column, row, row),
        in_specs=[FAST, pl.BlockSpec(memory_space=pltpu.SMEM)],
        out_specs=(FAST,) * 4,
        compiler_params=LIMIT,
        cost_estimate=cost(4 * 10**8),
        name="weights",
    )(offsets, pick)


def fast_call(kernel, name, out_shape, *operands):
    many = isinstance(out_shape, tuple)
    return pl.pallas_call(
        kernel,
        out_shape=out_shape,
        in_specs=[FAST] * len(operands),
        out_specs=(FAST,) * len(out_shape) if many else FAST,
        compiler_params=LIMIT,
        cost_estimate=cost(10**6),
        name=name,
    )(*operands)


def change_kernel(places, count, fill, own_ref, *refs):
    others = refs[: 1 if count == 2 else 2]
    next_out, prev_out, value = refs[-4 - fill :][:3]
    sem = refs[-1]
    position = lax.axis_index("die")
    for out, there, forward in (
        (next_out, position < count - 1, True),
        (prev_out, position > 0, False),
    ):

        @pl.when(there)
        def _():
            own = own_ref[...]
            value[...] = others[0][...] - own if forward else own - others[-1][...]
            copies = [
                pltpu.make_async_copy(
                    value.at[pl.ds(row, tall), pl.ds(column, wide)],
                    out.at[0, pl.ds(out_row, tall), pl.ds(out_column, wide)],
                    sem.at[k],
                )
                for k, ((row, column), (out_row, out_column), (tall, wide)) in enumerate(places)
            ]
            for copy in copies:
                copy.start()
            for copy in copies:
                copy.wait()

        if fill:

            @pl.when(jnp.logical_not(there))
            def _():
                zeros = refs[-2]
                zeros[...] = jnp.zeros_like(zeros)
                copy = pltpu.make_async_copy(zeros, out.at[0], sem.at[0])
                copy.start()
                copy.wait()


def change_call(count, places, flops, own, others, maps):
    operands = (own, *others)
    fill = not maps
    out = f32(1, TH, TW)
    return pl.pallas_call(
        functools.partial(change_kernel, places, count, fill),
        out_shape=(out, out),
        in_specs=[FAST] * len(operands) + [SLOW] * len(maps),
        out_specs=(SLOW, SLOW),
        scratch_shapes=[
            pltpu.VMEM(own.shape, jnp.float32),
            *([pltpu.VMEM((TH, TW), jnp.float32)] if fill else []),
            pltpu.SemaphoreType.DMA((len(places),)),
        ],
        input_output_aliases={len(operands) + k: k for k in range(len(maps))},
        compiler_params=LIMIT,
        cost_estimate=cost(flops),
        name="change",
    )(*operands, *maps)


LEAD_PLACES = (((0, 0), (FRAME, LANE), (LEAD, CORE)),)
REST_PLACES = (((0, 0), (FRAME + LEAD, LANE), (REST, CORE)),)
SIDE_PLACES = (((0, 0), (FRAME, 0), (MID, LANE)), ((0, LANE), (FRAME, TW - LANE), (MID, LANE)))
FRAME_PLACES = (((0, 0), (0, 0), (FRAME, TW)), ((FRAME, 0), (TH - FRAME, 0), (FRAME, TW)))


def swap_rounds(axis, first, second):
    count = lax.axis_size(axis)
    assert count % 2 == 0
    pairs = [(i, i ^ 1) for i in range(count)]
    others = [(i, min(max((i ^ 1) + 2 * (i % 2 * 2 - 1), 0), count - 1)) for i in range(count)]
    return lax.ppermute(first, axis, pairs), lax.ppermute(second, axis, others)


def other_dies(block):
    count = lax.axis_size("die")
    forward = [(i, i + 1) for i in range(count - 1)]
    backward = [(i + 1, i) for i in range(count - 1)]
    if count == 2:
        return (lax.ppermute(block, "die", forward + backward),)
    return (lax.ppermute(block, "die", backward), lax.ppermute(block, "die", forward))


def body(raster, shift_pick, offsets):
    count = lax.axis_size("die")
    weights = weights_call(offsets, shift_pick)
    lead, level = fast_call(lead_kernel, "lead", (f32(LEAD, CORE), f32(8, LANE)), raster, *weights)
    lead_others = other_dies(lead)
    strip = f32(FRAME, TH)
    rest, first, second = fast_call(rest_kernel, "rest", (f32(REST, CORE), strip, strip), raster, level, *weights)
    rest_others = other_dies(rest)
    first, second = swap_rounds("tx", first, second)
    halo = f32(FRAME, TW + LANE)
    side, send_first, send_second, edge = fast_call(
        side_kernel, "side", (f32(MID, 2 * LANE), halo, halo, f32(TH, LANE)), raster, level, first, second, *weights
    )
    side_others = other_dies(side)
    row_first, row_second = swap_rounds("ty", send_first, send_second)
    frame = fast_call(
        frame_kernel, "frame", f32(STRIP, TW), raster, level, edge, row_first, row_second, *weights
    )
    frame_others = other_dies(frame)
    maps = change_call(count, LEAD_PLACES, COSTS[0], lead, lead_others, ())
    maps = change_call(count, REST_PLACES, COSTS[1], rest, rest_others, maps)
    maps = change_call(count, SIDE_PLACES, COSTS[2], side, side_others, maps)
    return tuple(change_call(count, FRAME_PLACES, COSTS[3], frame, frame_others, maps))


def solution(mesh):
    in_specs = (P("die", "ty", "tx"), P("die", "ty", "tx"), P("die", "ty", "tx", None))
    out_specs = (P("die", "ty", "tx"), P("die", "ty", "tx"))
    return jax.shard_map(body, mesh=mesh, in_specs=in_specs, out_specs=out_specs, check_vma=False)
```

```python
import functools

import jax
import jax.numpy as jnp
import numpy as np
from jax import lax
from jax.experimental import pallas as pl
from jax.experimental.pallas import tpu as pltpu
from jax.sharding import PartitionSpec as P

TH = 256
TW = 1024
RG = 6
HW = 11
LANE = 128
FRAME = 16
STRIP = 2 * FRAME
CORE = TW - 2 * LANE
SPAN = 96
DEPTH = SPAN + 2 * FRAME
MID = TH - 2 * FRAME
LEAD = 96
REST = MID - LEAD
REACH = LANE + 2 * FRAME
BF16 = jnp.bfloat16


def gauss_taps(sigma):
    spots = np.arange(-RG, RG + 1).astype(np.float64)
    raw = np.exp(-spots * spots / (2.0 * sigma * sigma))
    return [float(tap) for tap in np.float32(raw / raw.sum())[RG:]]


NARROW = gauss_taps(1.0)
BROAD = gauss_taps(2.0)


def split(values):
    high = values.astype(BF16)
    low = (values - high.astype(jnp.float32)).astype(BF16)
    return high, low


def bands(distance, frac):
    def look(spots):
        away = jnp.abs(spots)
        narrow = jnp.zeros(spots.shape, jnp.float32)
        broad = jnp.zeros(spots.shape, jnp.float32)
        for tap in range(RG + 1):
            here = away == tap
            narrow = jnp.where(here, NARROW[tap], narrow)
            broad = jnp.where(here, BROAD[tap], broad)
        return narrow, broad

    near = look(distance)
    far = look(distance - 1)
    return tuple((1.0 - frac) * a + frac * b for a, b in zip(near, far))


def column_weights(offset, pick):
    frac = (pick // 4).astype(jnp.float32) * 0.5 + 0.25
    shape = (REACH, LANE)
    window = lax.broadcasted_iota(jnp.int32, shape, 0)
    result = lax.broadcasted_iota(jnp.int32, shape, 1)
    narrow, broad = bands(window - result - (HW + offset), frac)
    weights = split(jnp.concatenate([narrow, narrow - broad], axis=1))
    zeros = jnp.zeros((2 * LANE - REACH, 2 * LANE), BF16)
    return tuple(jnp.concatenate([half, zeros], axis=0) for half in weights)


def row_weights(offset, pick):
    frac = (pick % 4).astype(jnp.float32) * 0.25 + 0.125
    shape = (SPAN, DEPTH)
    source = lax.broadcasted_iota(jnp.int32, shape, 1)
    result = lax.broadcasted_iota(jnp.int32, shape, 0)
    narrow, broad = bands(source - result - (FRAME + offset), frac)
    return split(jnp.concatenate([narrow - broad, broad], axis=1))


def product(left, right):
    dot = functools.partial(jnp.dot, preferred_element_type=jnp.float32)
    return dot(left[0], right[0]) + (dot(left[1], right[0]) + dot(left[0], right[1]))


def column_sums(windows, column):
    rows = windows[0].shape[0]
    sums = split(product(split(jnp.concatenate(windows, axis=0)), column))
    blocks = [slice(k * rows, (k + 1) * rows) for k in range(len(windows))]
    return [
        [jnp.concatenate([half[block, part] for block in blocks], axis=1) for half in sums]
        for part in (slice(0, LANE), slice(LANE, 2 * LANE))
    ]


def row_sums(row, sums, first=0):
    narrow, change = sums
    short = DEPTH - (narrow[0].shape[0] - first)
    filler = [jnp.zeros((short, narrow[0].shape[1]), BF16)] if short > 0 else []
    rows = slice(first, first + DEPTH)
    stacked = [jnp.concatenate([a[rows], *filler, b[rows], *filler], axis=0) for a, b in zip(narrow, change)]
    return product(row, stacked)


def core_windows(values, level):
    rolled = pltpu.roll(values - level, HW, 1)
    return [rolled[:, block * LANE : (block + 2) * LANE] for block in range(1, TW // LANE - 1)]


def weights_kernel(off_ref, pick_ref, wh, wl, vh, vl):
    offsets = off_ref[0, 0]
    pick = pick_ref[0, 0, 0]
    wh[...], wl[...] = column_weights(offsets[:, 1:], pick)
    vh[...], vl[...] = row_weights(offsets[:, :1], pick)


def lead_kernel(x, wh, wl, vh, vl, lead, level_ref):
    total = jnp.sum(jnp.sum(x[0, :8, :], axis=0, keepdims=True), axis=1, keepdims=True)
    level = total * (1.0 / (8 * TW))
    level_ref[...] = jnp.broadcast_to(level, level_ref.shape)
    sums = column_sums(core_windows(x[0, : LEAD + 2 * FRAME, :], level), (wh[...], wl[...]))
    lead[...] = row_sums([half[:LEAD, :] for half in (vh, vl)], sums)


def rest_kernel(x, level_ref, wh, wl, vh, vl, rest, first, second):
    even = lax.axis_index("tx") % 2 == 0
    start = x[0, :, :LANE].T[:FRAME]
    end = x[0, :, TW - LANE :].T[LANE - FRAME :]
    first[...] = jnp.where(even, end, start)
    second[...] = jnp.where(even, start, end)
    column = (wh[...], wl[...])
    row = (vh[...], vl[...])
    sums = column_sums(core_windows(x[0, LEAD:, :], level_ref[:1, :1]), column)
    rest[:SPAN, :] = row_sums(row, sums)
    last = REST - SPAN
    lower = [half[SPAN - last :] for half in row]
    rest[SPAN:, :] = row_sums(lower, sums, TH - DEPTH - LEAD)


def halos(axis, first, second):
    place = lax.axis_index(axis)
    inner = (place > 0) & (place < lax.axis_size(axis) - 1)
    even = place % 2 == 0
    second = jnp.where(inner, second, 0.0)
    return jnp.where(even, second, first), jnp.where(even, first, second)


def side_kernel(x, level_ref, first, second, wh, wl, vh, vl, side, send_first, send_second, edge_ref):
    column = (wh[...], wl[...])
    row = (vh[...], vl[...])
    before, after = halos("tx", first[...], second[...])
    filler = jnp.zeros((LANE - 2 * FRAME, TH), jnp.float32)
    edge = jnp.concatenate([after, filler, before], axis=0).T
    edge_ref[...] = edge
    windows = [
        pltpu.roll(jnp.concatenate(strip, axis=1) - level_ref[:1, :1], 2 * LANE + HW, 1)[:, : 2 * LANE]
        for strip in ((edge, x[0, :, : 2 * LANE]), (x[0, :, TW - 2 * LANE :], edge))
    ]
    sums = column_sums(windows, column)
    side[:SPAN, :] = row_sums(row, sums)
    side[SPAN : 2 * SPAN, :] = row_sums(row, sums, SPAN)
    last = MID - 2 * SPAN
    lower = [half[SPAN - last :] for half in row]
    side[2 * SPAN :, :] = row_sums(lower, sums, TH - DEPTH)
    top = jnp.concatenate([x[0, :FRAME, :], edge[:FRAME]], axis=1)
    bottom = jnp.concatenate([x[0, TH - FRAME :, :], edge[TH - FRAME :]], axis=1)
    even = lax.axis_index("ty") % 2 == 0
    send_first[...] = jnp.where(even, bottom, top)
    send_second[...] = jnp.where(even, top, bottom)


def frame_kernel(x, level_ref, edge, row_first, row_second, wh, wl, vh, vl, frame):
    column = (wh[...], wl[...])
    top, bottom = halos("ty", row_first[...], row_second[...])
    own = [
        jnp.concatenate([x[0, rows, :], edge[rows, :]], axis=1)
        for rows in (slice(0, STRIP), slice(TH - STRIP, TH))
    ]
    values = jnp.concatenate([top, own[0], own[1], bottom], axis=0)
    rolled = pltpu.roll(values - level_ref[:1, :1], HW, 1)
    windows = [rolled[:, block * LANE : (block + 2) * LANE] for block in range(TW // LANE)]
    sums = column_sums(windows, column)
    below = values.shape[0] // 2
    row = [jnp.concatenate([half[:FRAME, :], half[below : below + FRAME, :]], axis=0) for half in (vh, vl)]
    frame[...] = row_sums(row, sums)


COSTS = (25 * 10**8, 10**10, 10**10, 10**10)
FAST = pl.BlockSpec(memory_space=pltpu.VMEM)
SLOW = pl.BlockSpec(memory_space=pltpu.HBM)
LIMIT = pltpu.CompilerParams(vmem_limit_bytes=16 * 2**20)


def f32(*shape):
    return jax.ShapeDtypeStruct(shape, jnp.float32)


def bf16(*shape):
    return jax.ShapeDtypeStruct(shape, BF16)


def cost(flops):
    return pl.CostEstimate(flops=flops, bytes_accessed=2**12, transcendentals=0)


def weights_call(offsets, pick):
    column = bf16(2 * LANE, 2 * LANE)
    row = bf16(SPAN, 2 * DEPTH)
    return pl.pallas_call(
        weights_kernel,
        out_shape=(column, column, row, row),
        in_specs=[FAST, pl.BlockSpec(memory_space=pltpu.SMEM)],
        out_specs=(FAST,) * 4,
        compiler_params=LIMIT,
        cost_estimate=cost(4 * 10**8),
        name="weights",
    )(offsets, pick)


def fast_call(kernel, name, out_shape, *operands):
    many = isinstance(out_shape, tuple)
    return pl.pallas_call(
        kernel,
        out_shape=out_shape,
        in_specs=[FAST] * len(operands),
        out_specs=(FAST,) * len(out_shape) if many else FAST,
        compiler_params=LIMIT,
        cost_estimate=cost(10**6),
        name=name,
    )(*operands)


def change_kernel(places, count, fill, own_ref, *refs):
    others = refs[: 1 if count == 2 else 2]
    next_out, prev_out, value = refs[-4 - fill :][:3]
    sem = refs[-1]
    position = lax.axis_index("die")
    for out, there, forward in (
        (next_out, position < count - 1, True),
        (prev_out, position > 0, False),
    ):

        @pl.when(there)
        def _():
            own = own_ref[...]
            value[...] = others[0][...] - own if forward else own - others[-1][...]
            copies = [
                pltpu.make_async_copy(
                    value.at[pl.ds(row, tall), pl.ds(column, wide)],
                    out.at[0, pl.ds(out_row, tall), pl.ds(out_column, wide)],
                    sem.at[k],
                )
                for k, ((row, column), (out_row, out_column), (tall, wide)) in enumerate(places)
            ]
            for copy in copies:
                copy.start()
            for copy in copies:
                copy.wait()

        if fill:

            @pl.when(jnp.logical_not(there))
            def _():
                zeros = refs[-2]
                zeros[...] = jnp.zeros_like(zeros)
                copy = pltpu.make_async_copy(zeros, out.at[0], sem.at[0])
                copy.start()
                copy.wait()


def change_call(count, places, flops, own, others, maps):
    operands = (own, *others)
    fill = not maps
    out = f32(1, TH, TW)
    return pl.pallas_call(
        functools.partial(change_kernel, places, count, fill),
        out_shape=(out, out),
        in_specs=[FAST] * len(operands) + [SLOW] * len(maps),
        out_specs=(SLOW, SLOW),
        scratch_shapes=[
            pltpu.VMEM(own.shape, jnp.float32),
            *([pltpu.VMEM((TH, TW), jnp.float32)] if fill else []),
            pltpu.SemaphoreType.DMA((len(places),)),
        ],
        input_output_aliases={len(operands) + k: k for k in range(len(maps))},
        compiler_params=LIMIT,
        cost_estimate=cost(flops),
        name="change",
    )(*operands, *maps)


LEAD_PLACES = (((0, 0), (FRAME, LANE), (LEAD, CORE)),)
REST_PLACES = (((0, 0), (FRAME + LEAD, LANE), (REST, CORE)),)
SIDE_PLACES = (((0, 0), (FRAME, 0), (MID, LANE)), ((0, LANE), (FRAME, TW - LANE), (MID, LANE)))
FRAME_PLACES = (((0, 0), (0, 0), (FRAME, TW)), ((FRAME, 0), (TH - FRAME, 0), (FRAME, TW)))


def swap_rounds(axis, first, second):
    count = lax.axis_size(axis)
    assert count % 2 == 0
    pairs = [(i, i ^ 1) for i in range(count)]
    others = [(i, min(max((i ^ 1) + 2 * (i % 2 * 2 - 1), 0), count - 1)) for i in range(count)]
    return lax.ppermute(first, axis, pairs), lax.ppermute(second, axis, others)


def other_dies(block):
    count = lax.axis_size("die")
    forward = [(i, i + 1) for i in range(count - 1)]
    backward = [(i + 1, i) for i in range(count - 1)]
    if count == 2:
        return (lax.ppermute(block, "die", forward + backward),)
    return (lax.ppermute(block, "die", backward), lax.ppermute(block, "die", forward))


def body(raster, shift_pick, offsets):
    count = lax.axis_size("die")
    weights = weights_call(offsets, shift_pick)
    lead, level = fast_call(lead_kernel, "lead", (f32(LEAD, CORE), f32(8, LANE)), raster, *weights)
    lead_others = other_dies(lead)
    strip = f32(FRAME, TH)
    rest, first, second = fast_call(rest_kernel, "rest", (f32(REST, CORE), strip, strip), raster, level, *weights)
    rest_others = other_dies(rest)
    first, second = swap_rounds("tx", first, second)
    halo = f32(FRAME, TW + LANE)
    side, send_first, send_second, edge = fast_call(
        side_kernel, "side", (f32(MID, 2 * LANE), halo, halo, f32(TH, LANE)), raster, level, first, second, *weights
    )
    side_others = other_dies(side)
    row_first, row_second = swap_rounds("ty", send_first, send_second)
    frame = fast_call(
        frame_kernel, "frame", f32(STRIP, TW), raster, level, edge, row_first, row_second, *weights
    )
    frame_others = other_dies(frame)
    maps = change_call(count, LEAD_PLACES, COSTS[0], lead, lead_others, ())
    maps = change_call(count, REST_PLACES, COSTS[1], rest, rest_others, maps)
    maps = change_call(count, SIDE_PLACES, COSTS[2], side, side_others, maps)
    return tuple(change_call(count, FRAME_PLACES, COSTS[3], frame, frame_others, maps))


def solution(mesh):
    in_specs = (P("die", "ty", "tx"), P("die", "ty", "tx"), P("die", "ty", "tx", None))
    out_specs = (P("die", "ty", "tx"), P("die", "ty", "tx"))
    return jax.shard_map(body, mesh=mesh, in_specs=in_specs, out_specs=out_specs, check_vma=False)
```

```python
import functools

import jax
import jax.numpy as jnp
import numpy as np
from jax import lax
from jax.experimental import pallas as pl
from jax.experimental.pallas import tpu as pltpu
from jax.sharding import PartitionSpec as P

TH = 256
TW = 1024
RG = 6
HW = 11
LANE = 128
FRAME = 16
STRIP = 2 * FRAME
CORE = TW - 2 * LANE
SPAN = 96
DEPTH = SPAN + 2 * FRAME
MID = TH - 2 * FRAME
LEAD = 48
REST = MID - LEAD
REACH = LANE + 2 * FRAME
BF16 = jnp.bfloat16


def gauss_taps(sigma):
    spots = np.arange(-RG, RG + 1).astype(np.float64)
    raw = np.exp(-spots * spots / (2.0 * sigma * sigma))
    return [float(tap) for tap in np.float32(raw / raw.sum())[RG:]]


NARROW = gauss_taps(1.0)
BROAD = gauss_taps(2.0)


def split(values):
    high = values.astype(BF16)
    low = (values - high.astype(jnp.float32)).astype(BF16)
    return high, low


def bands(distance, frac):
    def look(spots):
        away = jnp.abs(spots)
        narrow = jnp.zeros(spots.shape, jnp.float32)
        broad = jnp.zeros(spots.shape, jnp.float32)
        for tap in range(RG + 1):
            here = away == tap
            narrow = jnp.where(here, NARROW[tap], narrow)
            broad = jnp.where(here, BROAD[tap], broad)
        return narrow, broad

    near = look(distance)
    far = look(distance - 1)
    return tuple((1.0 - frac) * a + frac * b for a, b in zip(near, far))


def column_weights(offset, pick):
    frac = (pick // 4).astype(jnp.float32) * 0.5 + 0.25
    shape = (REACH, LANE)
    window = lax.broadcasted_iota(jnp.int32, shape, 0)
    result = lax.broadcasted_iota(jnp.int32, shape, 1)
    narrow, broad = bands(window - result - (HW + offset), frac)
    weights = split(jnp.concatenate([narrow, narrow - broad], axis=1))
    zeros = jnp.zeros((2 * LANE - REACH, 2 * LANE), BF16)
    return tuple(jnp.concatenate([half, zeros], axis=0) for half in weights)


def row_weights(offset, pick):
    frac = (pick % 4).astype(jnp.float32) * 0.25 + 0.125
    shape = (SPAN, DEPTH)
    source = lax.broadcasted_iota(jnp.int32, shape, 1)
    result = lax.broadcasted_iota(jnp.int32, shape, 0)
    narrow, broad = bands(source - result - (FRAME + offset), frac)
    return split(jnp.concatenate([narrow - broad, broad], axis=1))


def product(left, right):
    dot = functools.partial(jnp.dot, preferred_element_type=jnp.float32)
    return dot(left[0], right[0]) + (dot(left[1], right[0]) + dot(left[0], right[1]))


def column_sums(windows, column):
    rows = windows[0].shape[0]
    sums = split(product(split(jnp.concatenate(windows, axis=0)), column))
    blocks = [slice(k * rows, (k + 1) * rows) for k in range(len(windows))]
    return [
        [jnp.concatenate([half[block, part] for block in blocks], axis=1) for half in sums]
        for part in (slice(0, LANE), slice(LANE, 2 * LANE))
    ]


def row_sums(row, sums, first=0):
    narrow, change = sums
    short = DEPTH - (narrow[0].shape[0] - first)
    filler = [jnp.zeros((short, narrow[0].shape[1]), BF16)] if short > 0 else []
    rows = slice(first, first + DEPTH)
    stacked = [jnp.concatenate([a[rows], *filler, b[rows], *filler], axis=0) for a, b in zip(narrow, change)]
    return product(row, stacked)


def core_windows(values, level):
    rolled = pltpu.roll(values - level, HW, 1)
    return [rolled[:, block * LANE : (block + 2) * LANE] for block in range(1, TW // LANE - 1)]


def weights_kernel(off_ref, pick_ref, wh, wl, vh, vl):
    offsets = off_ref[0, 0]
    pick = pick_ref[0, 0, 0]
    wh[...], wl[...] = column_weights(offsets[:, 1:], pick)
    vh[...], vl[...] = row_weights(offsets[:, :1], pick)


def lead_kernel(x, wh, wl, vh, vl, lead, level_ref):
    total = jnp.sum(jnp.sum(x[0, :8, :], axis=0, keepdims=True), axis=1, keepdims=True)
    level = total * (1.0 / (8 * TW))
    level_ref[...] = jnp.broadcast_to(level, level_ref.shape)
    windows = core_windows(x[0, : LEAD + 2 * FRAME, :], level)
    column = (wh[...], wl[...])
    row = [half[:LEAD, :] for half in (vh, vl)]
    for group in range(0, len(windows), 2):
        spot = pl.ds(group * LANE, 2 * LANE)
        lead[:, spot] = row_sums(row, column_sums(windows[group : group + 2], column))


def rest_kernel(x, level_ref, wh, wl, vh, vl, rest, first, second):
    even = lax.axis_index("tx") % 2 == 0
    start = x[0, :, :LANE].T[:FRAME]
    end = x[0, :, TW - LANE :].T[LANE - FRAME :]
    first[...] = jnp.where(even, end, start)
    second[...] = jnp.where(even, start, end)
    column = (wh[...], wl[...])
    row = (vh[...], vl[...])
    sums = column_sums(core_windows(x[0, LEAD:, :], level_ref[:1, :1]), column)
    rest[:SPAN, :] = row_sums(row, sums)
    last = REST - SPAN
    lower = [half[SPAN - last :] for half in row]
    rest[SPAN:, :] = row_sums(lower, sums, TH - DEPTH - LEAD)


def halos(axis, first, second):
    place = lax.axis_index(axis)
    inner = (place > 0) & (place < lax.axis_size(axis) - 1)
    even = place % 2 == 0
    second = jnp.where(inner, second, 0.0)
    return jnp.where(even, second, first), jnp.where(even, first, second)


def side_kernel(x, level_ref, first, second, wh, wl, vh, vl, side, send_first, send_second, edge_ref):
    column = (wh[...], wl[...])
    row = (vh[...], vl[...])
    before, after = halos("tx", first[...], second[...])
    filler = jnp.zeros((LANE - 2 * FRAME, TH), jnp.float32)
    edge = jnp.concatenate([after, filler, before], axis=0).T
    edge_ref[...] = edge
    windows = [
        pltpu.roll(jnp.concatenate(strip, axis=1) - level_ref[:1, :1], 2 * LANE + HW, 1)[:, : 2 * LANE]
        for strip in ((edge, x[0, :, : 2 * LANE]), (x[0, :, TW - 2 * LANE :], edge))
    ]
    sums = column_sums(windows, column)
    side[:SPAN, :] = row_sums(row, sums)
    side[SPAN : 2 * SPAN, :] = row_sums(row, sums, SPAN)
    last = MID - 2 * SPAN
    lower = [half[SPAN - last :] for half in row]
    side[2 * SPAN :, :] = row_sums(lower, sums, TH - DEPTH)
    top = jnp.concatenate([x[0, :FRAME, :], edge[:FRAME]], axis=1)
    bottom = jnp.concatenate([x[0, TH - FRAME :, :], edge[TH - FRAME :]], axis=1)
    even = lax.axis_index("ty") % 2 == 0
    send_first[...] = jnp.where(even, bottom, top)
    send_second[...] = jnp.where(even, top, bottom)


def frame_kernel(x, level_ref, edge, row_first, row_second, wh, wl, vh, vl, frame):
    column = (wh[...], wl[...])
    top, bottom = halos("ty", row_first[...], row_second[...])
    own = [
        jnp.concatenate([x[0, rows, :], edge[rows, :]], axis=1)
        for rows in (slice(0, STRIP), slice(TH - STRIP, TH))
    ]
    values = jnp.concatenate([top, own[0], own[1], bottom], axis=0)
    rolled = pltpu.roll(values - level_ref[:1, :1], HW, 1)
    windows = [rolled[:, block * LANE : (block + 2) * LANE] for block in range(TW // LANE)]
    sums = column_sums(windows, column)
    below = values.shape[0] // 2
    row = [jnp.concatenate([half[:FRAME, :], half[below : below + FRAME, :]], axis=0) for half in (vh, vl)]
    frame[...] = row_sums(row, sums)


COSTS = (44 * 10**8, 10**10, 10**10, 10**10)
FAST = pl.BlockSpec(memory_space=pltpu.VMEM)
SLOW = pl.BlockSpec(memory_space=pltpu.HBM)
LIMIT = pltpu.CompilerParams(vmem_limit_bytes=16 * 2**20)


def f32(*shape):
    return jax.ShapeDtypeStruct(shape, jnp.float32)


def bf16(*shape):
    return jax.ShapeDtypeStruct(shape, BF16)


def cost(flops):
    return pl.CostEstimate(flops=flops, bytes_accessed=2**12, transcendentals=0)


def weights_call(offsets, pick):
    column = bf16(2 * LANE, 2 * LANE)
    row = bf16(SPAN, 2 * DEPTH)
    return pl.pallas_call(
        weights_kernel,
        out_shape=(column, column, row, row),
        in_specs=[FAST, pl.BlockSpec(memory_space=pltpu.SMEM)],
        out_specs=(FAST,) * 4,
        compiler_params=LIMIT,
        cost_estimate=cost(4 * 10**8),
        name="weights",
    )(offsets, pick)


def fast_call(kernel, name, out_shape, *operands):
    many = isinstance(out_shape, tuple)
    return pl.pallas_call(
        kernel,
        out_shape=out_shape,
        in_specs=[FAST] * len(operands),
        out_specs=(FAST,) * len(out_shape) if many else FAST,
        compiler_params=LIMIT,
        cost_estimate=cost(10**6),
        name=name,
    )(*operands)


def change_kernel(places, count, fill, own_ref, *refs):
    others = refs[: 1 if count == 2 else 2]
    next_out, prev_out, value = refs[-4 - fill :][:3]
    sem = refs[-1]
    position = lax.axis_index("die")
    for out, there, forward in (
        (next_out, position < count - 1, True),
        (prev_out, position > 0, False),
    ):

        @pl.when(there)
        def _():
            own = own_ref[...]
            value[...] = others[0][...] - own if forward else own - others[-1][...]
            copies = [
                pltpu.make_async_copy(
                    value.at[pl.ds(row, tall), pl.ds(column, wide)],
                    out.at[0, pl.ds(out_row, tall), pl.ds(out_column, wide)],
                    sem.at[k],
                )
                for k, ((row, column), (out_row, out_column), (tall, wide)) in enumerate(places)
            ]
            for copy in copies:
                copy.start()
            for copy in copies:
                copy.wait()

        if fill:

            @pl.when(jnp.logical_not(there))
            def _():
                zeros = refs[-2]
                zeros[...] = jnp.zeros_like(zeros)
                copy = pltpu.make_async_copy(zeros, out.at[0], sem.at[0])
                copy.start()
                copy.wait()


def change_call(count, places, flops, own, others, maps):
    operands = (own, *others)
    fill = not maps
    out = f32(1, TH, TW)
    return pl.pallas_call(
        functools.partial(change_kernel, places, count, fill),
        out_shape=(out, out),
        in_specs=[FAST] * len(operands) + [SLOW] * len(maps),
        out_specs=(SLOW, SLOW),
        scratch_shapes=[
            pltpu.VMEM(own.shape, jnp.float32),
            *([pltpu.VMEM((TH, TW), jnp.float32)] if fill else []),
            pltpu.SemaphoreType.DMA((len(places),)),
        ],
        input_output_aliases={len(operands) + k: k for k in range(len(maps))},
        compiler_params=LIMIT,
        cost_estimate=cost(flops),
        name="change",
    )(*operands, *maps)


LEAD_PLACES = (((0, 0), (FRAME, LANE), (LEAD, CORE)),)
REST_PLACES = (((0, 0), (FRAME + LEAD, LANE), (REST, CORE)),)
SIDE_PLACES = (((0, 0), (FRAME, 0), (MID, LANE)), ((0, LANE), (FRAME, TW - LANE), (MID, LANE)))
FRAME_PLACES = (((0, 0), (0, 0), (FRAME, TW)), ((FRAME, 0), (TH - FRAME, 0), (FRAME, TW)))


def swap_rounds(axis, first, second):
    count = lax.axis_size(axis)
    assert count % 2 == 0
    pairs = [(i, i ^ 1) for i in range(count)]
    others = [(i, min(max((i ^ 1) + 2 * (i % 2 * 2 - 1), 0), count - 1)) for i in range(count)]
    return lax.ppermute(first, axis, pairs), lax.ppermute(second, axis, others)


def other_dies(block):
    count = lax.axis_size("die")
    forward = [(i, i + 1) for i in range(count - 1)]
    backward = [(i + 1, i) for i in range(count - 1)]
    if count == 2:
        return (lax.ppermute(block, "die", forward + backward),)
    return (lax.ppermute(block, "die", backward), lax.ppermute(block, "die", forward))


def body(raster, shift_pick, offsets):
    count = lax.axis_size("die")
    weights = weights_call(offsets, shift_pick)
    lead, level = fast_call(lead_kernel, "lead", (f32(LEAD, CORE), f32(8, LANE)), raster, *weights)
    lead_others = other_dies(lead)
    strip = f32(FRAME, TH)
    rest, first, second = fast_call(rest_kernel, "rest", (f32(REST, CORE), strip, strip), raster, level, *weights)
    rest_others = other_dies(rest)
    first, second = swap_rounds("tx", first, second)
    halo = f32(FRAME, TW + LANE)
    side, send_first, send_second, edge = fast_call(
        side_kernel, "side", (f32(MID, 2 * LANE), halo, halo, f32(TH, LANE)), raster, level, first, second, *weights
    )
    side_others = other_dies(side)
    row_first, row_second = swap_rounds("ty", send_first, send_second)
    frame = fast_call(
        frame_kernel, "frame", f32(STRIP, TW), raster, level, edge, row_first, row_second, *weights
    )
    frame_others = other_dies(frame)
    maps = change_call(count, LEAD_PLACES, COSTS[0], lead, lead_others, ())
    maps = change_call(count, REST_PLACES, COSTS[1], rest, rest_others, maps)
    maps = change_call(count, SIDE_PLACES, COSTS[2], side, side_others, maps)
    return tuple(change_call(count, FRAME_PLACES, COSTS[3], frame, frame_others, maps))


def solution(mesh):
    in_specs = (P("die", "ty", "tx"), P("die", "ty", "tx"), P("die", "ty", "tx", None))
    out_specs = (P("die", "ty", "tx"), P("die", "ty", "tx"))
    return jax.shard_map(body, mesh=mesh, in_specs=in_specs, out_specs=out_specs, check_vma=False)
```

```python
import functools

import jax
import jax.numpy as jnp
import numpy as np
from jax import lax
from jax.experimental import pallas as pl
from jax.experimental.pallas import tpu as pltpu
from jax.sharding import PartitionSpec as P

TH = 256
TW = 1024
RG = 6
HW = 11
LANE = 128
FRAME = 16
STRIP = 2 * FRAME
CORE = TW - 2 * LANE
SPAN = 96
DEPTH = SPAN + 2 * FRAME
MID = TH - 2 * FRAME
LEAD = 64
REST = MID - LEAD
REACH = LANE + 2 * FRAME
BF16 = jnp.bfloat16


def gauss_taps(sigma):
    spots = np.arange(-RG, RG + 1).astype(np.float64)
    raw = np.exp(-spots * spots / (2.0 * sigma * sigma))
    return [float(tap) for tap in np.float32(raw / raw.sum())[RG:]]


NARROW = gauss_taps(1.0)
BROAD = gauss_taps(2.0)


def split(values):
    high = values.astype(BF16)
    low = (values - high.astype(jnp.float32)).astype(BF16)
    return high, low


def bands(distance, frac):
    def look(spots):
        away = jnp.abs(spots)
        narrow = jnp.zeros(spots.shape, jnp.float32)
        broad = jnp.zeros(spots.shape, jnp.float32)
        for tap in range(RG + 1):
            here = away == tap
            narrow = jnp.where(here, NARROW[tap], narrow)
            broad = jnp.where(here, BROAD[tap], broad)
        return narrow, broad

    near = look(distance)
    far = look(distance - 1)
    return tuple((1.0 - frac) * a + frac * b for a, b in zip(near, far))


def column_weights(offset, pick):
    frac = (pick // 4).astype(jnp.float32) * 0.5 + 0.25
    shape = (REACH, LANE)
    window = lax.broadcasted_iota(jnp.int32, shape, 0)
    result = lax.broadcasted_iota(jnp.int32, shape, 1)
    narrow, broad = bands(window - result - (HW + offset), frac)
    weights = split(jnp.concatenate([narrow, narrow - broad], axis=1))
    zeros = jnp.zeros((2 * LANE - REACH, 2 * LANE), BF16)
    return tuple(jnp.concatenate([half, zeros], axis=0) for half in weights)


def row_weights(offset, pick):
    frac = (pick % 4).astype(jnp.float32) * 0.25 + 0.125
    shape = (SPAN, DEPTH)
    source = lax.broadcasted_iota(jnp.int32, shape, 1)
    result = lax.broadcasted_iota(jnp.int32, shape, 0)
    narrow, broad = bands(source - result - (FRAME + offset), frac)
    return split(jnp.concatenate([narrow - broad, broad], axis=1))


def product(left, right):
    dot = functools.partial(jnp.dot, preferred_element_type=jnp.float32)
    return dot(left[0], right[0]) + (dot(left[1], right[0]) + dot(left[0], right[1]))


def column_sums(windows, column):
    rows = windows[0].shape[0]
    sums = split(product(split(jnp.concatenate(windows, axis=0)), column))
    blocks = [slice(k * rows, (k + 1) * rows) for k in range(len(windows))]
    return [
        [jnp.concatenate([half[block, part] for block in blocks], axis=1) for half in sums]
        for part in (slice(0, LANE), slice(LANE, 2 * LANE))
    ]


def row_sums(row, sums, first=0):
    narrow, change = sums
    short = DEPTH - (narrow[0].shape[0] - first)
    filler = [jnp.zeros((short, narrow[0].shape[1]), BF16)] if short > 0 else []
    rows = slice(first, first + DEPTH)
    stacked = [jnp.concatenate([a[rows], *filler, b[rows], *filler], axis=0) for a, b in zip(narrow, change)]
    return product(row, stacked)


def core_windows(values, level):
    rolled = pltpu.roll(values - level, HW, 1)
    return [rolled[:, block * LANE : (block + 2) * LANE] for block in range(1, TW // LANE - 1)]


def weights_kernel(off_ref, pick_ref, wh, wl, vh, vl):
    offsets = off_ref[0, 0]
    pick = pick_ref[0, 0, 0]
    wh[...], wl[...] = column_weights(offsets[:, 1:], pick)
    vh[...], vl[...] = row_weights(offsets[:, :1], pick)


def lead_kernel(x, wh, wl, vh, vl, lead, level_ref):
    blocks = [x[0, :8, k * LANE : (k + 1) * LANE] for k in range(TW // LANE)]
    total = jnp.sum(jnp.sum(sum(blocks[1:], blocks[0]), axis=0, keepdims=True), axis=1, keepdims=True)
    level = total * (1.0 / (8 * TW))
    level_ref[...] = jnp.broadcast_to(level, level_ref.shape)
    sums = column_sums(core_windows(x[0, : LEAD + 2 * FRAME, :], level), (wh[...], wl[...]))
    lead[...] = row_sums([half[:LEAD, :] for half in (vh, vl)], sums)


def rest_kernel(x, level_ref, wh, wl, vh, vl, rest, first, second):
    even = lax.axis_index("tx") % 2 == 0
    start = x[0, :, :LANE].T[:FRAME]
    end = x[0, :, TW - LANE :].T[LANE - FRAME :]
    first[...] = jnp.where(even, end, start)
    second[...] = jnp.where(even, start, end)
    column = (wh[...], wl[...])
    row = (vh[...], vl[...])
    sums = column_sums(core_windows(x[0, LEAD:, :], level_ref[:1, :1]), column)
    rest[:SPAN, :] = row_sums(row, sums)
    last = REST - SPAN
    lower = [half[SPAN - last :] for half in row]
    rest[SPAN:, :] = row_sums(lower, sums, TH - DEPTH - LEAD)


def halos(axis, first, second):
    place = lax.axis_index(axis)
    inner = (place > 0) & (place < lax.axis_size(axis) - 1)
    even = place % 2 == 0
    second = jnp.where(inner, second, 0.0)
    return jnp.where(even, second, first), jnp.where(even, first, second)


def side_kernel(x, level_ref, first, second, wh, wl, vh, vl, side, send_first, send_second, edge_ref):
    column = (wh[...], wl[...])
    row = (vh[...], vl[...])
    before, after = halos("tx", first[...], second[...])
    filler = jnp.zeros((LANE - 2 * FRAME, TH), jnp.float32)
    edge = jnp.concatenate([after, filler, before], axis=0).T
    edge_ref[...] = edge
    windows = [
        pltpu.roll(jnp.concatenate(strip, axis=1) - level_ref[:1, :1], 2 * LANE + HW, 1)[:, : 2 * LANE]
        for strip in ((edge, x[0, :, : 2 * LANE]), (x[0, :, TW - 2 * LANE :], edge))
    ]
    sums = column_sums(windows, column)
    side[:SPAN, :] = row_sums(row, sums)
    side[SPAN : 2 * SPAN, :] = row_sums(row, sums, SPAN)
    last = MID - 2 * SPAN
    lower = [half[SPAN - last :] for half in row]
    side[2 * SPAN :, :] = row_sums(lower, sums, TH - DEPTH)
    top = jnp.concatenate([x[0, :FRAME, :], edge[:FRAME]], axis=1)
    bottom = jnp.concatenate([x[0, TH - FRAME :, :], edge[TH - FRAME :]], axis=1)
    even = lax.axis_index("ty") % 2 == 0
    send_first[...] = jnp.where(even, bottom, top)
    send_second[...] = jnp.where(even, top, bottom)


def frame_kernel(x, level_ref, edge, row_first, row_second, wh, wl, vh, vl, frame):
    column = (wh[...], wl[...])
    top, bottom = halos("ty", row_first[...], row_second[...])
    own = [
        jnp.concatenate([x[0, rows, :], edge[rows, :]], axis=1)
        for rows in (slice(0, STRIP), slice(TH - STRIP, TH))
    ]
    values = jnp.concatenate([top, own[0], own[1], bottom], axis=0)
    rolled = pltpu.roll(values - level_ref[:1, :1], HW, 1)
    windows = [rolled[:, block * LANE : (block + 2) * LANE] for block in range(TW // LANE)]
    sums = column_sums(windows, column)
    below = values.shape[0] // 2
    row = [jnp.concatenate([half[:FRAME, :], half[below : below + FRAME, :]], axis=0) for half in (vh, vl)]
    frame[...] = row_sums(row, sums)


COSTS = (39 * 10**8, 10**10, 10**10, 10**10)
FAST = pl.BlockSpec(memory_space=pltpu.VMEM)
SLOW = pl.BlockSpec(memory_space=pltpu.HBM)
LIMIT = pltpu.CompilerParams(vmem_limit_bytes=16 * 2**20)


def f32(*shape):
    return jax.ShapeDtypeStruct(shape, jnp.float32)


def bf16(*shape):
    return jax.ShapeDtypeStruct(shape, BF16)


def cost(flops):
    return pl.CostEstimate(flops=flops, bytes_accessed=2**12, transcendentals=0)


def weights_call(offsets, pick):
    column = bf16(2 * LANE, 2 * LANE)
    row = bf16(SPAN, 2 * DEPTH)
    return pl.pallas_call(
        weights_kernel,
        out_shape=(column, column, row, row),
        in_specs=[FAST, pl.BlockSpec(memory_space=pltpu.SMEM)],
        out_specs=(FAST,) * 4,
        compiler_params=LIMIT,
        cost_estimate=cost(4 * 10**8),
        name="weights",
    )(offsets, pick)


def fast_call(kernel, name, out_shape, *operands):
    many = isinstance(out_shape, tuple)
    return pl.pallas_call(
        kernel,
        out_shape=out_shape,
        in_specs=[FAST] * len(operands),
        out_specs=(FAST,) * len(out_shape) if many else FAST,
        compiler_params=LIMIT,
        cost_estimate=cost(10**6),
        name=name,
    )(*operands)


def change_kernel(places, count, fill, own_ref, *refs):
    others = refs[: 1 if count == 2 else 2]
    next_out, prev_out, value = refs[-4 - fill :][:3]
    sem = refs[-1]
    position = lax.axis_index("die")
    for out, there, forward in (
        (next_out, position < count - 1, True),
        (prev_out, position > 0, False),
    ):

        @pl.when(there)
        def _():
            copies = []
            for k, ((row, column), (out_row, out_column), (tall, wide)) in enumerate(places):
                rows, columns = pl.ds(row, tall), pl.ds(column, wide)
                own = own_ref[rows, columns]
                other = others[0 if forward else -1][rows, columns]
                value[rows, columns] = other - own if forward else own - other
                copies.append(
                    pltpu.make_async_copy(
                        value.at[rows, columns],
                        out.at[0, pl.ds(out_row, tall), pl.ds(out_column, wide)],
                        sem.at[k],
                    )
                )
                copies[-1].start()
            for copy in copies:
                copy.wait()

        if fill:

            @pl.when(jnp.logical_not(there))
            def _():
                zeros = refs[-2]
                zeros[...] = jnp.zeros_like(zeros)
                copy = pltpu.make_async_copy(zeros, out.at[0], sem.at[0])
                copy.start()
                copy.wait()


def change_call(count, places, flops, own, others, maps):
    operands = (own, *others)
    fill = not maps
    out = f32(1, TH, TW)
    return pl.pallas_call(
        functools.partial(change_kernel, places, count, fill),
        out_shape=(out, out),
        in_specs=[FAST] * len(operands) + [SLOW] * len(maps),
        out_specs=(SLOW, SLOW),
        scratch_shapes=[
            pltpu.VMEM(own.shape, jnp.float32),
            *([pltpu.VMEM((TH, TW), jnp.float32)] if fill else []),
            pltpu.SemaphoreType.DMA((len(places),)),
        ],
        input_output_aliases={len(operands) + k: k for k in range(len(maps))},
        compiler_params=LIMIT,
        cost_estimate=cost(flops),
        name="change",
    )(*operands, *maps)


LEAD_PLACES = (((0, 0), (FRAME, LANE), (LEAD, CORE)),)
REST_PLACES = (((0, 0), (FRAME + LEAD, LANE), (REST, CORE)),)
SIDE_PLACES = (((0, 0), (FRAME, 0), (MID, LANE)), ((0, LANE), (FRAME, TW - LANE), (MID, LANE)))
FRAME_PLACES = (((0, 0), (0, 0), (FRAME, TW)), ((FRAME, 0), (TH - FRAME, 0), (FRAME, TW)))


def swap_rounds(axis, first, second):
    count = lax.axis_size(axis)
    assert count % 2 == 0
    pairs = [(i, i ^ 1) for i in range(count)]
    others = [(i, min(max((i ^ 1) + 2 * (i % 2 * 2 - 1), 0), count - 1)) for i in range(count)]
    return lax.ppermute(first, axis, pairs), lax.ppermute(second, axis, others)


def other_dies(block):
    count = lax.axis_size("die")
    forward = [(i, i + 1) for i in range(count - 1)]
    backward = [(i + 1, i) for i in range(count - 1)]
    if count == 2:
        return (lax.ppermute(block, "die", forward + backward),)
    return (lax.ppermute(block, "die", backward), lax.ppermute(block, "die", forward))


def body(raster, shift_pick, offsets):
    count = lax.axis_size("die")
    weights = weights_call(offsets, shift_pick)
    lead, level = fast_call(lead_kernel, "lead", (f32(LEAD, CORE), f32(8, LANE)), raster, *weights)
    lead_others = other_dies(lead)
    strip = f32(FRAME, TH)
    rest, first, second = fast_call(rest_kernel, "rest", (f32(REST, CORE), strip, strip), raster, level, *weights)
    rest_others = other_dies(rest)
    first, second = swap_rounds("tx", first, second)
    halo = f32(FRAME, TW + LANE)
    side, send_first, send_second, edge = fast_call(
        side_kernel, "side", (f32(MID, 2 * LANE), halo, halo, f32(TH, LANE)), raster, level, first, second, *weights
    )
    side_others = other_dies(side)
    row_first, row_second = swap_rounds("ty", send_first, send_second)
    frame = fast_call(
        frame_kernel, "frame", f32(STRIP, TW), raster, level, edge, row_first, row_second, *weights
    )
    frame_others = other_dies(frame)
    maps = change_call(count, LEAD_PLACES, COSTS[0], lead, lead_others, ())
    maps = change_call(count, REST_PLACES, COSTS[1], rest, rest_others, maps)
    maps = change_call(count, SIDE_PLACES, COSTS[2], side, side_others, maps)
    return tuple(change_call(count, FRAME_PLACES, COSTS[3], frame, frame_others, maps))


def solution(mesh):
    in_specs = (P("die", "ty", "tx"), P("die", "ty", "tx"), P("die", "ty", "tx", None))
    out_specs = (P("die", "ty", "tx"), P("die", "ty", "tx"))
    return jax.shard_map(body, mesh=mesh, in_specs=in_specs, out_specs=out_specs, check_vma=False)
```

```python
import functools

import jax
import jax.numpy as jnp
import numpy as np
from jax import lax
from jax.experimental import pallas as pl
from jax.experimental.pallas import tpu as pltpu
from jax.sharding import PartitionSpec as P

TH = 256
TW = 1024
RG = 6
HW = 11
LANE = 128
FRAME = 16
STRIP = 2 * FRAME
CORE = TW - 2 * LANE
SPAN = 96
DEPTH = SPAN + 2 * FRAME
MID = TH - 2 * FRAME
LEAD = 48
REST = MID - LEAD
REACH = LANE + 2 * FRAME
BF16 = jnp.bfloat16


def gauss_taps(sigma):
    spots = np.arange(-RG, RG + 1).astype(np.float64)
    raw = np.exp(-spots * spots / (2.0 * sigma * sigma))
    return [float(tap) for tap in np.float32(raw / raw.sum())[RG:]]


NARROW = gauss_taps(1.0)
BROAD = gauss_taps(2.0)


def split(values):
    high = values.astype(BF16)
    low = (values - high.astype(jnp.float32)).astype(BF16)
    return high, low


def bands(distance, frac):
    def look(spots):
        away = jnp.abs(spots)
        narrow = jnp.zeros(spots.shape, jnp.float32)
        broad = jnp.zeros(spots.shape, jnp.float32)
        for tap in range(RG + 1):
            here = away == tap
            narrow = jnp.where(here, NARROW[tap], narrow)
            broad = jnp.where(here, BROAD[tap], broad)
        return narrow, broad

    near = look(distance)
    far = look(distance - 1)
    return tuple((1.0 - frac) * a + frac * b for a, b in zip(near, far))


def column_weights(offset, pick):
    frac = (pick // 4).astype(jnp.float32) * 0.5 + 0.25
    shape = (REACH, LANE)
    window = lax.broadcasted_iota(jnp.int32, shape, 0)
    result = lax.broadcasted_iota(jnp.int32, shape, 1)
    narrow, broad = bands(window - result - (HW + offset), frac)
    weights = split(jnp.concatenate([narrow, narrow - broad], axis=1))
    zeros = jnp.zeros((2 * LANE - REACH, 2 * LANE), BF16)
    return tuple(jnp.concatenate([half, zeros], axis=0) for half in weights)


def row_weights(offset, pick):
    frac = (pick % 4).astype(jnp.float32) * 0.25 + 0.125
    shape = (SPAN, DEPTH)
    source = lax.broadcasted_iota(jnp.int32, shape, 1)
    result = lax.broadcasted_iota(jnp.int32, shape, 0)
    narrow, broad = bands(source - result - (FRAME + offset), frac)
    return split(jnp.concatenate([narrow - broad, broad], axis=1))


def product(left, right):
    dot = functools.partial(jnp.dot, preferred_element_type=jnp.float32)
    return dot(left[0], right[0]) + (dot(left[1], right[0]) + dot(left[0], right[1]))


def column_sums(windows, column):
    rows = windows[0].shape[0]
    sums = split(product(split(jnp.concatenate(windows, axis=0)), column))
    blocks = [slice(k * rows, (k + 1) * rows) for k in range(len(windows))]
    return [
        [jnp.concatenate([half[block, part] for block in blocks], axis=1) for half in sums]
        for part in (slice(0, LANE), slice(LANE, 2 * LANE))
    ]


def row_sums(row, sums, first=0):
    narrow, change = sums
    short = DEPTH - (narrow[0].shape[0] - first)
    filler = [jnp.zeros((short, narrow[0].shape[1]), BF16)] if short > 0 else []
    rows = slice(first, first + DEPTH)
    stacked = [jnp.concatenate([a[rows], *filler, b[rows], *filler], axis=0) for a, b in zip(narrow, change)]
    return product(row, stacked)


def core_windows(values, level):
    rolled = pltpu.roll(values - level, HW, 1)
    return [rolled[:, block * LANE : (block + 2) * LANE] for block in range(1, TW // LANE - 1)]


def weights_kernel(off_ref, pick_ref, wh, wl, vh, vl):
    offsets = off_ref[0, 0]
    pick = pick_ref[0, 0, 0]
    wh[...], wl[...] = column_weights(offsets[:, 1:], pick)
    vh[...], vl[...] = row_weights(offsets[:, :1], pick)


def lead_kernel(x, wh, wl, vh, vl, lead, level_ref):
    blocks = [x[0, :8, k * LANE : (k + 1) * LANE] for k in range(TW // LANE)]
    total = jnp.sum(jnp.sum(sum(blocks[1:], blocks[0]), axis=0, keepdims=True), axis=1, keepdims=True)
    level = total * (1.0 / (8 * TW))
    level_ref[...] = jnp.broadcast_to(level, level_ref.shape)
    sums = column_sums(core_windows(x[0, : LEAD + 2 * FRAME, :], level), (wh[...], wl[...]))
    lead[...] = row_sums([half[:LEAD, :] for half in (vh, vl)], sums)


def rest_kernel(x, level_ref, wh, wl, vh, vl, rest, first, second):
    even = lax.axis_index("tx") % 2 == 0
    start = x[0, :, :LANE].T[:FRAME]
    end = x[0, :, TW - LANE :].T[LANE - FRAME :]
    first[...] = jnp.where(even, end, start)
    second[...] = jnp.where(even, start, end)
    column = (wh[...], wl[...])
    row = (vh[...], vl[...])
    sums = column_sums(core_windows(x[0, LEAD:, :], level_ref[:1, :1]), column)
    rest[:SPAN, :] = row_sums(row, sums)
    last = REST - SPAN
    lower = [half[SPAN - last :] for half in row]
    rest[SPAN:, :] = row_sums(lower, sums, TH - DEPTH - LEAD)


def halos(axis, first, second):
    place = lax.axis_index(axis)
    inner = (place > 0) & (place < lax.axis_size(axis) - 1)
    even = place % 2 == 0
    second = jnp.where(inner, second, 0.0)
    return jnp.where(even, second, first), jnp.where(even, first, second)


def side_kernel(x, level_ref, first, second, wh, wl, vh, vl, side, send_first, send_second, edge_ref):
    column = (wh[...], wl[...])
    row = (vh[...], vl[...])
    before, after = halos("tx", first[...], second[...])
    filler = jnp.zeros((LANE - 2 * FRAME, TH), jnp.float32)
    edge = jnp.concatenate([after, filler, before], axis=0).T
    edge_ref[...] = edge
    windows = [
        pltpu.roll(jnp.concatenate(strip, axis=1) - level_ref[:1, :1], 2 * LANE + HW, 1)[:, : 2 * LANE]
        for strip in ((edge, x[0, :, : 2 * LANE]), (x[0, :, TW - 2 * LANE :], edge))
    ]
    sums = column_sums(windows, column)
    side[:SPAN, :] = row_sums(row, sums)
    side[SPAN : 2 * SPAN, :] = row_sums(row, sums, SPAN)
    last = MID - 2 * SPAN
    lower = [half[SPAN - last :] for half in row]
    side[2 * SPAN :, :] = row_sums(lower, sums, TH - DEPTH)
    top = jnp.concatenate([x[0, :FRAME, :], edge[:FRAME]], axis=1)
    bottom = jnp.concatenate([x[0, TH - FRAME :, :], edge[TH - FRAME :]], axis=1)
    even = lax.axis_index("ty") % 2 == 0
    send_first[...] = jnp.where(even, bottom, top)
    send_second[...] = jnp.where(even, top, bottom)


def frame_kernel(x, level_ref, edge, row_first, row_second, wh, wl, vh, vl, frame):
    column = (wh[...], wl[...])
    top, bottom = halos("ty", row_first[...], row_second[...])
    own = [
        jnp.concatenate([x[0, rows, :], edge[rows, :]], axis=1)
        for rows in (slice(0, STRIP), slice(TH - STRIP, TH))
    ]
    values = jnp.concatenate([top, own[0], own[1], bottom], axis=0)
    rolled = pltpu.roll(values - level_ref[:1, :1], HW, 1)
    windows = [rolled[:, block * LANE : (block + 2) * LANE] for block in range(TW // LANE)]
    sums = column_sums(windows, column)
    below = values.shape[0] // 2
    row = [jnp.concatenate([half[:FRAME, :], half[below : below + FRAME, :]], axis=0) for half in (vh, vl)]
    frame[...] = row_sums(row, sums)


COSTS = (44 * 10**8, 10**10, 10**10, 10**10)
FAST = pl.BlockSpec(memory_space=pltpu.VMEM)
SLOW = pl.BlockSpec(memory_space=pltpu.HBM)
LIMIT = pltpu.CompilerParams(vmem_limit_bytes=16 * 2**20)


def f32(*shape):
    return jax.ShapeDtypeStruct(shape, jnp.float32)


def bf16(*shape):
    return jax.ShapeDtypeStruct(shape, BF16)


def cost(flops):
    return pl.CostEstimate(flops=flops, bytes_accessed=2**12, transcendentals=0)


def weights_call(offsets, pick):
    column = bf16(2 * LANE, 2 * LANE)
    row = bf16(SPAN, 2 * DEPTH)
    return pl.pallas_call(
        weights_kernel,
        out_shape=(column, column, row, row),
        in_specs=[FAST, pl.BlockSpec(memory_space=pltpu.SMEM)],
        out_specs=(FAST,) * 4,
        compiler_params=LIMIT,
        cost_estimate=cost(4 * 10**8),
        name="weights",
    )(offsets, pick)


def fast_call(kernel, name, out_shape, *operands):
    many = isinstance(out_shape, tuple)
    return pl.pallas_call(
        kernel,
        out_shape=out_shape,
        in_specs=[FAST] * len(operands),
        out_specs=(FAST,) * len(out_shape) if many else FAST,
        compiler_params=LIMIT,
        cost_estimate=cost(10**6),
        name=name,
    )(*operands)


def change_kernel(places, count, fill, own_ref, *refs):
    others = refs[: 1 if count == 2 else 2]
    next_out, prev_out, value = refs[-4 - fill :][:3]
    sem = refs[-1]
    position = lax.axis_index("die")
    for out, there, forward in (
        (next_out, position < count - 1, True),
        (prev_out, position > 0, False),
    ):

        @pl.when(there)
        def _():
            copies = []
            for k, ((row, column), (out_row, out_column), (tall, wide)) in enumerate(places):
                rows, columns = pl.ds(row, tall), pl.ds(column, wide)
                own = own_ref[rows, columns]
                other = others[0 if forward else -1][rows, columns]
                value[rows, columns] = other - own if forward else own - other
                copies.append(
                    pltpu.make_async_copy(
                        value.at[rows, columns],
                        out.at[0, pl.ds(out_row, tall), pl.ds(out_column, wide)],
                        sem.at[k],
                    )
                )
                copies[-1].start()
            for copy in copies:
                copy.wait()

        if fill:

            @pl.when(jnp.logical_not(there))
            def _():
                zeros = refs[-2]
                zeros[...] = jnp.zeros_like(zeros)
                copy = pltpu.make_async_copy(zeros, out.at[0], sem.at[0])
                copy.start()
                copy.wait()


def change_call(count, places, flops, own, others, maps):
    operands = (own, *others)
    fill = not maps
    out = f32(1, TH, TW)
    return pl.pallas_call(
        functools.partial(change_kernel, places, count, fill),
        out_shape=(out, out),
        in_specs=[FAST] * len(operands) + [SLOW] * len(maps),
        out_specs=(SLOW, SLOW),
        scratch_shapes=[
            pltpu.VMEM(own.shape, jnp.float32),
            *([pltpu.VMEM((TH, TW), jnp.float32)] if fill else []),
            pltpu.SemaphoreType.DMA((len(places),)),
        ],
        input_output_aliases={len(operands) + k: k for k in range(len(maps))},
        compiler_params=LIMIT,
        cost_estimate=cost(flops),
        name="change",
    )(*operands, *maps)


LEAD_PLACES = (((0, 0), (FRAME, LANE), (LEAD, CORE)),)
REST_PLACES = (((0, 0), (FRAME + LEAD, LANE), (REST, CORE)),)
SIDE_PLACES = (((0, 0), (FRAME, 0), (MID, LANE)), ((0, LANE), (FRAME, TW - LANE), (MID, LANE)))
FRAME_PLACES = (((0, 0), (0, 0), (FRAME, TW)), ((FRAME, 0), (TH - FRAME, 0), (FRAME, TW)))


def swap_rounds(axis, first, second):
    count = lax.axis_size(axis)
    assert count % 2 == 0
    pairs = [(i, i ^ 1) for i in range(count)]
    others = [(i, min(max((i ^ 1) + 2 * (i % 2 * 2 - 1), 0), count - 1)) for i in range(count)]
    return lax.ppermute(first, axis, pairs), lax.ppermute(second, axis, others)


def other_dies(block):
    count = lax.axis_size("die")
    forward = [(i, i + 1) for i in range(count - 1)]
    backward = [(i + 1, i) for i in range(count - 1)]
    if count == 2:
        return (lax.ppermute(block, "die", forward + backward),)
    return (lax.ppermute(block, "die", backward), lax.ppermute(block, "die", forward))


def body(raster, shift_pick, offsets):
    count = lax.axis_size("die")
    weights = weights_call(offsets, shift_pick)
    lead, level = fast_call(lead_kernel, "lead", (f32(LEAD, CORE), f32(8, LANE)), raster, *weights)
    lead_others = other_dies(lead)
    strip = f32(FRAME, TH)
    rest, first, second = fast_call(rest_kernel, "rest", (f32(REST, CORE), strip, strip), raster, level, *weights)
    rest_others = other_dies(rest)
    first, second = swap_rounds("tx", first, second)
    halo = f32(FRAME, TW + LANE)
    side, send_first, send_second, edge = fast_call(
        side_kernel, "side", (f32(MID, 2 * LANE), halo, halo, f32(TH, LANE)), raster, level, first, second, *weights
    )
    side_others = other_dies(side)
    row_first, row_second = swap_rounds("ty", send_first, send_second)
    frame = fast_call(
        frame_kernel, "frame", f32(STRIP, TW), raster, level, edge, row_first, row_second, *weights
    )
    frame_others = other_dies(frame)
    maps = change_call(count, LEAD_PLACES, COSTS[0], lead, lead_others, ())
    maps = change_call(count, REST_PLACES, COSTS[1], rest, rest_others, maps)
    maps = change_call(count, SIDE_PLACES, COSTS[2], side, side_others, maps)
    return tuple(change_call(count, FRAME_PLACES, COSTS[3], frame, frame_others, maps))


def solution(mesh):
    in_specs = (P("die", "ty", "tx"), P("die", "ty", "tx"), P("die", "ty", "tx", None))
    out_specs = (P("die", "ty", "tx"), P("die", "ty", "tx"))
    return jax.shard_map(body, mesh=mesh, in_specs=in_specs, out_specs=out_specs, check_vma=False)
```

```python
import functools

import jax
import jax.numpy as jnp
import numpy as np
from jax import lax
from jax.experimental import pallas as pl
from jax.experimental.pallas import tpu as pltpu
from jax.sharding import PartitionSpec as P

TH = 256
TW = 1024
RG = 6
HW = 11
LANE = 128
FRAME = 16
STRIP = 2 * FRAME
CORE = TW - 2 * LANE
SPAN = 96
DEPTH = SPAN + 2 * FRAME
MID = TH - 2 * FRAME
LEAD = 48
REST = MID - LEAD
REACH = LANE + 2 * FRAME
BF16 = jnp.bfloat16


def gauss_taps(sigma):
    spots = np.arange(-RG, RG + 1).astype(np.float64)
    raw = np.exp(-spots * spots / (2.0 * sigma * sigma))
    return [float(tap) for tap in np.float32(raw / raw.sum())[RG:]]


NARROW = gauss_taps(1.0)
BROAD = gauss_taps(2.0)


def split(values):
    high = values.astype(BF16)
    low = (values - high.astype(jnp.float32)).astype(BF16)
    return high, low


def bands(distance, frac):
    def look(spots):
        away = jnp.abs(spots)
        narrow = jnp.zeros(spots.shape, jnp.float32)
        broad = jnp.zeros(spots.shape, jnp.float32)
        for tap in range(RG + 1):
            here = away == tap
            narrow = jnp.where(here, NARROW[tap], narrow)
            broad = jnp.where(here, BROAD[tap], broad)
        return narrow, broad

    near = look(distance)
    far = look(distance - 1)
    return tuple((1.0 - frac) * a + frac * b for a, b in zip(near, far))


def column_weights(offset, pick):
    frac = (pick // 4).astype(jnp.float32) * 0.5 + 0.25
    shape = (REACH, LANE)
    window = lax.broadcasted_iota(jnp.int32, shape, 0)
    result = lax.broadcasted_iota(jnp.int32, shape, 1)
    narrow, broad = bands(window - result - (HW + offset), frac)
    weights = split(jnp.concatenate([narrow, narrow - broad], axis=1))
    zeros = jnp.zeros((2 * LANE - REACH, 2 * LANE), BF16)
    return tuple(jnp.concatenate([half, zeros], axis=0) for half in weights)


def row_weights(offset, pick):
    frac = (pick % 4).astype(jnp.float32) * 0.25 + 0.125
    shape = (SPAN, DEPTH)
    source = lax.broadcasted_iota(jnp.int32, shape, 1)
    result = lax.broadcasted_iota(jnp.int32, shape, 0)
    narrow, broad = bands(source - result - (FRAME + offset), frac)
    return split(jnp.concatenate([narrow - broad, broad], axis=1))


def product(left, right):
    dot = functools.partial(jnp.dot, preferred_element_type=jnp.float32)
    return dot(left[0], right[0]) + (dot(left[1], right[0]) + dot(left[0], right[1]))


def column_sums(windows, column):
    rows = windows[0].shape[0]
    sums = split(product(split(jnp.concatenate(windows, axis=0)), column))
    blocks = [slice(k * rows, (k + 1) * rows) for k in range(len(windows))]
    return [
        [jnp.concatenate([half[block, part] for block in blocks], axis=1) for half in sums]
        for part in (slice(0, LANE), slice(LANE, 2 * LANE))
    ]


def row_sums(row, sums, first=0):
    narrow, change = sums
    short = DEPTH - (narrow[0].shape[0] - first)
    filler = [jnp.zeros((short, narrow[0].shape[1]), BF16)] if short > 0 else []
    rows = slice(first, first + DEPTH)
    stacked = [jnp.concatenate([a[rows], *filler, b[rows], *filler], axis=0) for a, b in zip(narrow, change)]
    return product(row, stacked)


def core_windows(values, level):
    rolled = pltpu.roll(values - level, HW, 1)
    return [rolled[:, block * LANE : (block + 2) * LANE] for block in range(1, TW // LANE - 1)]


def weights_kernel(off_ref, pick_ref, wh, wl, vh, vl):
    offsets = off_ref[0, 0]
    pick = pick_ref[0, 0, 0]
    wh[...], wl[...] = column_weights(offsets[:, 1:], pick)
    vh[...], vl[...] = row_weights(offsets[:, :1], pick)


def lead_kernel(x, wh, wl, vh, vl, lead, level_ref):
    total = jnp.sum(jnp.sum(x[0, :8, :], axis=0, keepdims=True), axis=1, keepdims=True)
    level = total * (1.0 / (8 * TW))
    level_ref[...] = jnp.broadcast_to(level, level_ref.shape)
    sums = column_sums(core_windows(x[0, : LEAD + 2 * FRAME, :], level), (wh[...], wl[...]))
    lead[...] = row_sums([half[:LEAD, :] for half in (vh, vl)], sums)


def rest_kernel(x, level_ref, wh, wl, vh, vl, rest, first, second):
    even = lax.axis_index("tx") % 2 == 0
    start = x[0, :, :LANE].T[:FRAME]
    end = x[0, :, TW - LANE :].T[LANE - FRAME :]
    first[...] = jnp.where(even, end, start)
    second[...] = jnp.where(even, start, end)
    column = (wh[...], wl[...])
    row = (vh[...], vl[...])
    sums = column_sums(core_windows(x[0, LEAD:, :], level_ref[:1, :1]), column)
    rest[:SPAN, :] = row_sums(row, sums)
    last = REST - SPAN
    lower = [half[SPAN - last :] for half in row]
    rest[SPAN:, :] = row_sums(lower, sums, TH - DEPTH - LEAD)


def halos(axis, first, second):
    place = lax.axis_index(axis)
    inner = (place > 0) & (place < lax.axis_size(axis) - 1)
    even = place % 2 == 0
    second = jnp.where(inner, second, 0.0)
    return jnp.where(even, second, first), jnp.where(even, first, second)


def side_kernel(x, level_ref, first, second, wh, wl, vh, vl, side, send_first, send_second, edge_ref):
    column = (wh[...], wl[...])
    row = (vh[...], vl[...])
    before, after = halos("tx", first[...], second[...])
    filler = jnp.zeros((LANE - 2 * FRAME, TH), jnp.float32)
    edge = jnp.concatenate([after, filler, before], axis=0).T
    edge_ref[...] = edge
    windows = [
        pltpu.roll(jnp.concatenate(strip, axis=1) - level_ref[:1, :1], 2 * LANE + HW, 1)[:, : 2 * LANE]
        for strip in ((edge, x[0, :, : 2 * LANE]), (x[0, :, TW - 2 * LANE :], edge))
    ]
    sums = column_sums(windows, column)
    side[:SPAN, :] = row_sums(row, sums)
    side[SPAN : 2 * SPAN, :] = row_sums(row, sums, SPAN)
    last = MID - 2 * SPAN
    lower = [half[SPAN - last :] for half in row]
    side[2 * SPAN :, :] = row_sums(lower, sums, TH - DEPTH)
    top = jnp.concatenate([x[0, :FRAME, :], edge[:FRAME]], axis=1)
    bottom = jnp.concatenate([x[0, TH - FRAME :, :], edge[TH - FRAME :]], axis=1)
    even = lax.axis_index("ty") % 2 == 0
    send_first[...] = jnp.where(even, bottom, top)
    send_second[...] = jnp.where(even, top, bottom)


def frame_kernel(x, level_ref, edge, row_first, row_second, wh, wl, vh, vl, frame):
    column = (wh[...], wl[...])
    top, bottom = halos("ty", row_first[...], row_second[...])
    own = [
        jnp.concatenate([x[0, rows, :], edge[rows, :]], axis=1)
        for rows in (slice(0, STRIP), slice(TH - STRIP, TH))
    ]
    values = jnp.concatenate([top, own[0], own[1], bottom], axis=0)
    rolled = pltpu.roll(values - level_ref[:1, :1], HW, 1)
    windows = [rolled[:, block * LANE : (block + 2) * LANE] for block in range(TW // LANE)]
    sums = column_sums(windows, column)
    below = values.shape[0] // 2
    row = [jnp.concatenate([half[:FRAME, :], half[below : below + FRAME, :]], axis=0) for half in (vh, vl)]
    frame[...] = row_sums(row, sums)


COSTS = (44 * 10**8, 10**10, 10**10, 10**10)
FAST = pl.BlockSpec(memory_space=pltpu.VMEM)
SLOW = pl.BlockSpec(memory_space=pltpu.HBM)
LIMIT = pltpu.CompilerParams(vmem_limit_bytes=16 * 2**20)


def f32(*shape):
    return jax.ShapeDtypeStruct(shape, jnp.float32)


def bf16(*shape):
    return jax.ShapeDtypeStruct(shape, BF16)


def cost(flops):
    return pl.CostEstimate(flops=flops, bytes_accessed=2**12, transcendentals=0)


def weights_call(offsets, pick):
    column = bf16(2 * LANE, 2 * LANE)
    row = bf16(SPAN, 2 * DEPTH)
    return pl.pallas_call(
        weights_kernel,
        out_shape=(column, column, row, row),
        in_specs=[FAST, pl.BlockSpec(memory_space=pltpu.SMEM)],
        out_specs=(FAST,) * 4,
        compiler_params=LIMIT,
        cost_estimate=cost(4 * 10**8),
        name="weights",
    )(offsets, pick)


def fast_call(kernel, name, out_shape, *operands):
    many = isinstance(out_shape, tuple)
    return pl.pallas_call(
        kernel,
        out_shape=out_shape,
        in_specs=[FAST] * len(operands),
        out_specs=(FAST,) * len(out_shape) if many else FAST,
        compiler_params=LIMIT,
        cost_estimate=cost(10**6),
        name=name,
    )(*operands)


def change_kernel(places, count, fill, own_ref, *refs):
    others = refs[: 1 if count == 2 else 2]
    next_out, prev_out, value = refs[-4 - fill :][:3]
    sem = refs[-1]
    position = lax.axis_index("die")
    for out, there, forward in (
        (next_out, position < count - 1, True),
        (prev_out, position > 0, False),
    ):

        @pl.when(there)
        def _():
            copies = []
            for k, ((row, column), (out_row, out_column), (tall, wide)) in enumerate(places):
                rows, columns = pl.ds(row, tall), pl.ds(column, wide)
                own = own_ref[rows, columns]
                other = others[0 if forward else -1][rows, columns]
                value[rows, columns] = other - own if forward else own - other
                copies.append(
                    pltpu.make_async_copy(
                        value.at[rows, columns],
                        out.at[0, pl.ds(out_row, tall), pl.ds(out_column, wide)],
                        sem.at[k],
                    )
                )
                copies[-1].start()
            for copy in copies:
                copy.wait()

        if fill:

            @pl.when(jnp.logical_not(there))
            def _():
                zeros = refs[-2]
                zeros[...] = jnp.zeros_like(zeros)
                copy = pltpu.make_async_copy(zeros, out.at[0], sem.at[0])
                copy.start()
                copy.wait()


def change_call(count, places, flops, own, others, maps):
    operands = (own, *others)
    fill = not maps
    out = f32(1, TH, TW)
    return pl.pallas_call(
        functools.partial(change_kernel, places, count, fill),
        out_shape=(out, out),
        in_specs=[FAST] * len(operands) + [SLOW] * len(maps),
        out_specs=(SLOW, SLOW),
        scratch_shapes=[
            pltpu.VMEM(own.shape, jnp.float32),
            *([pltpu.VMEM((TH, TW), jnp.float32)] if fill else []),
            pltpu.SemaphoreType.DMA((len(places),)),
        ],
        input_output_aliases={len(operands) + k: k for k in range(len(maps))},
        compiler_params=LIMIT,
        cost_estimate=cost(flops),
        name="change",
    )(*operands, *maps)


LEAD_PLACES = (((0, 0), (FRAME, LANE), (LEAD, CORE)),)
REST_PLACES = (((0, 0), (FRAME + LEAD, LANE), (REST, CORE)),)
SIDE_PLACES = (((0, 0), (FRAME, 0), (MID, LANE)), ((0, LANE), (FRAME, TW - LANE), (MID, LANE)))
FRAME_PLACES = (((0, 0), (0, 0), (FRAME, TW)), ((FRAME, 0), (TH - FRAME, 0), (FRAME, TW)))


def swap_rounds(axis, first, second):
    count = lax.axis_size(axis)
    assert count % 2 == 0
    pairs = [(i, i ^ 1) for i in range(count)]
    others = [(i, min(max((i ^ 1) + 2 * (i % 2 * 2 - 1), 0), count - 1)) for i in range(count)]
    return lax.ppermute(first, axis, pairs), lax.ppermute(second, axis, others)


def other_dies(block):
    count = lax.axis_size("die")
    forward = [(i, i + 1) for i in range(count - 1)]
    backward = [(i + 1, i) for i in range(count - 1)]
    if count == 2:
        return (lax.ppermute(block, "die", forward + backward),)
    return (lax.ppermute(block, "die", backward), lax.ppermute(block, "die", forward))


def body(raster, shift_pick, offsets):
    count = lax.axis_size("die")
    weights = weights_call(offsets, shift_pick)
    lead, level = fast_call(lead_kernel, "lead", (f32(LEAD, CORE), f32(8, LANE)), raster, *weights)
    lead_others = other_dies(lead)
    strip = f32(FRAME, TH)
    rest, first, second = fast_call(rest_kernel, "rest", (f32(REST, CORE), strip, strip), raster, level, *weights)
    rest_others = other_dies(rest)
    first, second = swap_rounds("tx", first, second)
    halo = f32(FRAME, TW + LANE)
    side, send_first, send_second, edge = fast_call(
        side_kernel, "side", (f32(MID, 2 * LANE), halo, halo, f32(TH, LANE)), raster, level, first, second, *weights
    )
    side_others = other_dies(side)
    row_first, row_second = swap_rounds("ty", send_first, send_second)
    frame = fast_call(
        frame_kernel, "frame", f32(STRIP, TW), raster, level, edge, row_first, row_second, *weights
    )
    frame_others = other_dies(frame)
    maps = change_call(count, LEAD_PLACES, COSTS[0], lead, lead_others, ())
    maps = change_call(count, REST_PLACES, COSTS[1], rest, rest_others, maps)
    maps = change_call(count, SIDE_PLACES, COSTS[2], side, side_others, maps)
    return tuple(change_call(count, FRAME_PLACES, COSTS[3], frame, frame_others, maps))


def solution(mesh):
    in_specs = (P("die", "ty", "tx"), P("die", "ty", "tx"), P("die", "ty", "tx", None))
    out_specs = (P("die", "ty", "tx"), P("die", "ty", "tx"))
    return jax.shard_map(body, mesh=mesh, in_specs=in_specs, out_specs=out_specs, check_vma=False)
```
